32 devices in a mesh: gx: 8 (over z, y), gy: 4 (over x, core).
Axes of the slice: x: 2, y: 2, z: 4, core: 2. Of those that a mesh axis runs over, the one named last changes fastest.
Arguments:
- actuator_mask: int32 [8, 32, 32, 128], P(None, 'gx', 'gy'), may hold values 0 or 1
- forcing: float32 [8, 4, 32, 32, 128], P(None, None, 'gx', 'gy'), may hold values from -18 to 18
- base_flow: float32 [3, 32, 32, 128], P(None, 'gx', 'gy'), may hold values from -0.3 to 0.3
- base_shear: float32 [3, 3, 32, 32, 128], P(None, None, 'gx', 'gy'), may hold values from -1.5 to 1.5
Outputs:
- q_basis: float32 [72, 4, 32, 32, 128], P(None, None, 'gx', 'gy')
- r_factor: float32 [72, 72], replicated
- column_rms: float32 [72], replicated
The draws below stay inside these ranges and needn't reach their ends.
All inputs are finite; a program needn't handle non-finite values. No bound on the sum of `actuator_mask` on one device may be relied on, other than what follows from the above.
Results may differ from the reference program's by a relative error of at most 0.004.
Values sent between devices are 32-bit elements; how exact they have to be, the bound alone decides.
A program may use at most 64 MiB of HBM per device.

```python
import jax
import jax.numpy as jnp
from jax import lax

RHS = 8
S = 8
COLS = 72
NX = 32
NY = 32
NZ = 128


def draw_forcing(key, part):
    position = jnp.arange(NX, dtype=jnp.float32) / max(NX - 1, 1)
    values = jax.random.truncated_normal(key, -3.0, 3.0, (RHS, 4, NX, NY, NZ), jnp.float32)
    scale = 1.0 + 4.0 * position
    return values * scale[None, None, :, None, None]


def set_ends(entries, stream_key, low, largest):
    longest = entries.shape.index(max(entries.shape))
    spots = []
    for shift in (0, 1):
        where = [jax.random.randint(jax.random.fold_in(stream_key, axis), (), 0, length) for axis, length in enumerate(entries.shape)]
        where[longest] = (where[longest] + shift) % entries.shape[longest]
        spots.append(tuple(where))
    return entries.at[spots[0]].set(low).at[spots[1]].set(largest)


def block_scale(own_key, shape, split, least, top_value):
    def one(dim, blocks):
        steps = jax.random.uniform(jax.random.fold_in(jax.random.fold_in(own_key, 6), dim), (blocks,), jnp.float32, least / len(split), top_value / len(split))
        return jnp.repeat(jnp.exp(steps), shape[dim] // blocks).reshape((-1,) + (1,) * (len(shape) - dim - 1))

    loudness = one(*split[0])
    for cut in split[1:]:
        loudness = loudness * one(*cut)
    return loudness


def noise(own_key, dims, deviation, limit, shards=(), held_as=jnp.bfloat16):
    array = deviation * jax.random.normal(own_key, dims, jnp.float32)
    if shards:
        array = array * block_scale(own_key, dims, shards, -0.22, 0.18)
    return jnp.clip(array, -limit, limit).astype(held_as)


def setup_inputs(seed: int = 0) -> dict:
    keys = jax.random.split(jax.random.key(seed), 5)
    return {
        "actuator_mask": set_ends((jax.random.randint(keys[0], (RHS, NX, NY, NZ), 0, 2) < 1).astype(jnp.int32), jax.random.fold_in(keys[0], 1), 0, 1),
        "forcing": draw_forcing(jax.random.fold_in(keys[4], 71), 0),
        "base_flow": jnp.clip(jax.random.uniform(keys[2], (3, NX, NY, NZ), jnp.float32, -0.3, 0.3) * block_scale(keys[2], (3, NX, NY, NZ), ((1, 8), (2, 4)), -0.4, 0.0), -0.3, 0.3),
        "base_shear": noise(keys[3], (3, 3, NX, NY, NZ), 0.3, 1.5, ((2, 8), (3, 4)), jnp.float32),
    }


viscosity = 0.04
diffusivity = 0.04
coupling = 0.5
spectral_shift = 0.5

def operate_core(padded, coefficients):
    centre = padded[:, :, 1:-1, 1:-1, 1:-1]
    x_plus = padded[:, :, 2:, 1:-1, 1:-1]
    x_minus = padded[:, :, :-2, 1:-1, 1:-1]
    y_plus = padded[:, :, 1:-1, 2:, 1:-1]
    y_minus = padded[:, :, 1:-1, :-2, 1:-1]
    z_plus = padded[:, :, 1:-1, 1:-1, 2:]
    z_minus = padded[:, :, 1:-1, 1:-1, :-2]
    laplace = x_plus + x_minus + y_plus + y_minus + z_plus + z_minus - 6.0 * centre
    slopes = [0.5 * (x_plus - x_minus), 0.5 * (y_plus - y_minus), 0.5 * (z_plus - z_minus)]
    velocity = centre[:, :3]
    velocity_out = viscosity * laplace[:, :3] - spectral_shift * velocity
    for component in range(3):
        velocity_out = velocity_out - coefficients[component][None, None] * slopes[component][:, :3]
        velocity_out = velocity_out - coefficients[3 + component:12:3][None] * velocity[:, component:component + 1]
    pressure_grad = jnp.stack([slopes[component][:, 3] for component in range(3)], axis=1)
    velocity_out = velocity_out - pressure_grad
    divergence = slopes[0][:, 0] + slopes[1][:, 1] + slopes[2][:, 2]
    pressure_out = diffusivity * laplace[:, 3] - coupling * divergence - spectral_shift * centre[:, 3]
    return jnp.concatenate([velocity_out, pressure_out[:, None]], axis=1)

def reference(actuator_mask, forcing, base_flow, base_shear):
    coefficients = jnp.concatenate([base_flow, base_shear.reshape(9, NX, NY, NZ)], axis=0)
    column = forcing * actuator_mask[:, None].astype(jnp.float32)
    krylov = [column]
    for section in range(S):
        padded = jnp.pad(column, ((0, 0), (0, 0), (1, 1), (1, 1), (1, 1)))
        column = operate_core(padded, coefficients)
        krylov.append(column)
    stacked = jnp.stack(krylov, axis=1)
    matrix = stacked.reshape(COLS, -1)
    column_rms = jnp.sqrt(lax.optimization_barrier(jnp.sum(matrix * matrix, axis=1)) / (4.0 * NX * NY * NZ))
    q_factor, r_factor = jnp.linalg.qr(matrix.T)
    sign_flip = jnp.where(jnp.diagonal(r_factor) < 0, -1.0, 1.0).astype(jnp.float32)
    q_factor = q_factor * sign_flip[None]
    r_factor = r_factor * sign_flip[:, None]
    return (q_factor.T.reshape(COLS, 4, NX, NY, NZ), r_factor, column_rms)
```

```python
import functools

import jax
import jax.numpy as jnp
import numpy as np
from jax import lax
from jax.experimental import pallas as pl
from jax.experimental.pallas import tpu as pltpu
from jax.sharding import PartitionSpec as P

S = 8
RHS = 8
STEPS = S + 1
COLS = RHS * STEPS
VMEM = pltpu.VMEM
MESH = pl.DeviceIdType.MESH
HIGHEST = lax.Precision.HIGHEST

viscosity = 0.04
diffusivity = 0.04
coupling = 0.5
spectral_shift = 0.5

SHIFT = -(6.0 * viscosity + spectral_shift)
BACK = 0.2


def change_of_basis():
    hessenberg = np.zeros((STEPS, STEPS))
    for k in range(STEPS):
        hessenberg[k, k] = SHIFT
        if k + 1 < STEPS:
            hessenberg[k + 1, k] = 1.0
        if k > 0:
            hessenberg[k - 1, k] = -BACK
    change = np.zeros((STEPS, STEPS))
    column = np.zeros(STEPS)
    column[0] = 1.0
    for k in range(STEPS):
        change[:, k] = column
        column = hessenberg @ column
    return change


def place(order):
    source, k = divmod(order, STEPS)
    return k * RHS + source


def output_constants():
    change = change_of_basis()
    permute = np.zeros((COLS, COLS), np.float32)
    mix = np.zeros((COLS, COLS), np.float32)
    for i in range(COLS):
        permute[i, place(i)] = 1.0
    for r in range(RHS):
        for a in range(STEPS):
            for b in range(STEPS):
                mix[a * RHS + r, r * STEPS + b] = change[a, b]
    return permute, mix


def split3(value):
    high = value.astype(jnp.bfloat16)
    rest = value - high.astype(jnp.float32)
    middle = rest.astype(jnp.bfloat16)
    low = (rest - middle.astype(jnp.float32)).astype(jnp.bfloat16)
    return high, middle, low


def basis_kernel(
    counts, cells,
    mask_ref, forcing_ref, flow_ref, shear_ref,
    basis_ref, inverse_ref, factor_ref,
    fields, gram, one, two,
    send_x, recv_x, send_y, recv_y, send_one, recv_one, send_two, recv_two, save_sem,
):
    count_x, count_y = counts
    cells_x, cells_y = cells
    gx = lax.axis_index("gx")
    gy = lax.axis_index("gy")

    barrier = pltpu.get_barrier_semaphore()
    for step in range(1, count_x):
        pl.semaphore_signal(
            barrier, inc=1, device_id=(lax.rem(gx + step, count_x), gy), device_id_type=MESH
        )
    for step in range(1, count_y):
        pl.semaphore_signal(
            barrier, inc=1, device_id=(gx, lax.rem(gy + step, count_y)), device_id_type=MESH
        )

    zero = jnp.zeros((8, 128), jnp.float32)
    lane = lax.broadcasted_iota(jnp.int32, (8, 128), 1)
    first_lane, last_lane = lane == 0, lane == 127

    def clear(k, carry):
        @pl.when(gx == 0)
        def _():
            fields[k, :, 0] = jnp.zeros(fields.shape[1:2] + fields.shape[3:], jnp.float32)

        @pl.when(gx == count_x - 1)
        def _():
            fields[k, :, cells_x + 1] = jnp.zeros(
                fields.shape[1:2] + fields.shape[3:], jnp.float32
            )

        @pl.when(gy == 0)
        def _():
            fields[k, :, :, 0] = jnp.zeros(fields.shape[1:3] + fields.shape[4:], jnp.float32)

        @pl.when(gy == count_y - 1)
        def _():
            fields[k, :, :, cells_y + 1] = jnp.zeros(
                fields.shape[1:3] + fields.shape[4:], jnp.float32
            )

        return carry

    lax.fori_loop(1, STEPS, clear, 0)
    fields[0] = jnp.zeros(fields.shape[1:], jnp.float32)

    def start_row(i, carry):
        x, y = i // cells_y, lax.rem(i, cells_y)
        mask = mask_ref[pl.ds(i, RHS, stride=cells_x * cells_y), :].astype(jnp.float32)
        for f in range(4):
            where = f * cells_x * cells_y + i
            value = forcing_ref[pl.ds(where, RHS, stride=4 * cells_x * cells_y), :]
            fields[1, f, x + 1, y + 1] = value * mask
        return carry

    lax.fori_loop(0, cells_x * cells_y, start_row, 0)
    pl.semaphore_wait(barrier, count_x + count_y - 2)

    def halo(k, axis, up):
        side = 1 if up else 0
        if axis == 0:
            source = cells_x if up else 1
            target = 0 if up else cells_x + 1
            rows = pl.ds(1, cells_y)
            return pltpu.make_async_remote_copy(
                src_ref=fields.at[k, :, source, rows],
                dst_ref=fields.at[k, :, target, rows],
                send_sem=send_x.at[k, side],
                recv_sem=recv_x.at[k, side],
                device_id=(gx + 1 if up else gx - 1, gy),
                device_id_type=MESH,
            )
        source = cells_y if up else 1
        target = 0 if up else cells_y + 1
        rows = pl.ds(1, cells_x)
        return pltpu.make_async_remote_copy(
            src_ref=fields.at[k, :, rows, source],
            dst_ref=fields.at[k, :, rows, target],
            send_sem=send_y.at[k, side],
            recv_sem=recv_y.at[k, side],
            device_id=(gx, gy + 1 if up else gy - 1),
            device_id_type=MESH,
        )

    def at_sides(k, axis, what):
        me, count = (gx, count_x) if axis == 0 else (gy, count_y)
        for up in (True, False):
            sends = me < count - 1 if up else me > 0
            receives = me > 0 if up else me < count - 1

            @pl.when(receives if what == "recv" else sends)
            def _(up=up):
                copy = halo(k, axis, up)
                if what == "start":
                    copy.start()
                elif what == "send":
                    copy.wait_send()
                else:
                    copy.wait_recv()

    def advance(k, x, y):
        def value(f, dx=0, dy=0):
            return fields[k, f, x + 1 + dx, y + 1 + dy]

        centre = [value(f) for f in range(4)]
        plus = [
            [value(f, 1, 0) for f in range(4)],
            [value(f, 0, 1) for f in range(4)],
            [jnp.where(last_lane, zero, pltpu.roll(centre[f], 127, 1)) for f in range(4)],
        ]
        minus = [
            [value(f, -1, 0) for f in range(4)],
            [value(f, 0, -1) for f in range(4)],
            [jnp.where(first_lane, zero, pltpu.roll(centre[f], 1, 1)) for f in range(4)],
        ]
        result = [BACK * fields[k - 1, f, x + 1, y + 1] for f in range(4)]
        for j in range(3):
            half = 0.5 * flow_ref[j, x, pl.ds(y, 1), :]
            ahead = jnp.broadcast_to(viscosity - half, (8, 128))
            behind = jnp.broadcast_to(viscosity + half, (8, 128))
            for i in range(3):
                result[i] = result[i] + ahead * plus[j][i] + behind * minus[j][i]
                shear = jnp.broadcast_to(shear_ref[i, j, x, pl.ds(y, 1), :], (8, 128))
                result[i] = result[i] - shear * centre[j]
            result[j] = result[j] - 0.5 * (plus[j][3] - minus[j][3])
            result[3] = result[3] + diffusivity * (plus[j][3] + minus[j][3])
            result[3] = result[3] - (0.5 * coupling) * (plus[j][j] - minus[j][j])
        for f in range(4):
            fields[k + 1, f, x + 1, y + 1] = result[f]

    def save(k):
        return pltpu.make_async_copy(
            fields.at[k, :, pl.ds(1, cells_x), pl.ds(1, cells_y)],
            basis_ref.at[:, :, :, pl.ds(pl.multiple_of((k - 1) * RHS, RHS), RHS)],
            save_sem.at[k],
        )

    def section(k, carry):
        def x_faces(y, carry):
            advance(k, 0, y)
            advance(k, cells_x - 1, y)
            return carry

        def y_faces(x, carry):
            advance(k, x, 0)
            advance(k, x, cells_y - 1)
            return carry

        def inside(y, carry):
            for x in range(1, cells_x - 1):
                advance(k, x, y)
            return carry

        at_sides(k, 0, "recv")
        at_sides(k, 1, "recv")
        lax.fori_loop(0, cells_y, x_faces, 0)

        @pl.when(k < S)
        def _():
            at_sides(k + 1, 0, "start")

        lax.fori_loop(1, cells_x - 1, y_faces, 0)

        @pl.when(k < S)
        def _():
            at_sides(k + 1, 1, "start")

        lax.fori_loop(1, cells_y - 1, inside, 0)
        save(k + 1).start()
        return carry

    at_sides(1, 0, "start")
    at_sides(1, 1, "start")
    save(1).start()
    lax.fori_loop(1, STEPS, section, 0)

    gram[...] = jnp.zeros_like(gram)
    padding = jnp.zeros((8, 128 * cells_y), jnp.float32)

    def accumulate(i, carry):
        f, x = i // cells_x, lax.rem(i, cells_x)
        block = jnp.concatenate(
            [
                jnp.concatenate([fields[k, f, x + 1, y + 1] for y in range(cells_y)], axis=1)
                for k in range(1, STEPS + 1)
            ]
            + [padding],
            axis=0,
        )
        parts = jnp.concatenate(split3(block), axis=0)
        gram[...] += lax.dot_general(
            parts, parts, (((1,), (1,)), ((), ())), preferred_element_type=jnp.float32
        )
        return carry

    lax.fori_loop(0, 4 * cells_x, accumulate, 0)
    height = COLS + 8
    own = gram[0:COLS, 0:COLS]
    for a in range(3):
        for b in range(3):
            if a or b:
                own = own + gram[a * height : a * height + COLS, b * height : b * height + COLS]
    own = jnp.concatenate([own, jnp.zeros((COLS, 128 - COLS), jnp.float32)], axis=1)

    def exchange(slots, me, count, device, send, recv):
        def copy(step, slot, partner):
            return pltpu.make_async_remote_copy(
                src_ref=slots.at[slot],
                dst_ref=slots.at[slot],
                send_sem=send.at[step],
                recv_sem=recv.at[step],
                device_id=device(partner),
                device_id_type=MESH,
            )

        for step in range(1, count):
            copy(step, me, lax.rem(me + step, count)).start()
        for step in range(1, count):
            source = lax.rem(me + count - step, count)
            copy(step, source, source).wait_recv()
        total = slots[0]
        for slot in range(1, count):
            total = total + slots[slot]
        for step in range(1, count):
            copy(step, me, lax.rem(me + step, count)).wait_send()
        return total

    one[gy] = own
    own = exchange(one, gy, count_y, lambda p: (gx, p), send_one, recv_one)
    two[gx] = own
    matrix = exchange(two, gx, count_x, lambda p: (p, gy), send_two, recv_two)

    rows = lax.broadcasted_iota(jnp.int32, (COLS, 128), 0)
    columns = lax.broadcasted_iota(jnp.int32, (COLS, 128), 1)
    rank = lax.rem(rows, RHS) * STEPS + rows // RHS
    column_rank = lax.rem(columns, RHS) * STEPS + columns // RHS
    inverse = jnp.where(rows == columns, 1.0, 0.0)
    for order in range(COLS):
        p = place(order)
        row = matrix[p : p + 1, :]
        inverse_row = inverse[p : p + 1, :]
        pivot = matrix[p : p + 1, p : p + 1]
        scale = lax.rsqrt(pivot)
        scale = scale * (1.5 - 0.5 * pivot * scale * scale)
        factor_ref[p : p + 1, :] = jnp.where(
            column_rank[0:1, :] >= order, row * scale, 0.0
        )
        inverse_ref[p : p + 1, :] = inverse_row * scale
        if order + 1 < COLS:
            multiple = matrix[:, p : p + 1] * (1.0 / pivot)
            multiple = jnp.where(rank > order, multiple, 0.0)
            matrix = matrix - multiple * row
            inverse = inverse - multiple * inverse_row

    def finish(k, carry):
        at_sides(k, 0, "send")
        at_sides(k, 1, "send")
        return carry

    lax.fori_loop(1, STEPS, finish, 0)
    for k in range(1, STEPS + 1):
        save(k).wait()


def basis(mask, forcing, flow, shear, counts):
    _, cells_x, cells_y, _ = flow.shape
    cells = (cells_x, cells_y)
    grid_cells = cells_x * cells_y
    count_x, count_y = counts
    height = COLS + 8
    dma = pltpu.SemaphoreType.DMA
    return pl.pallas_call(
        functools.partial(basis_kernel, counts, cells),
        out_shape=(
            jax.ShapeDtypeStruct((4, cells_x, cells_y, COLS, 128), jnp.float32),
            jax.ShapeDtypeStruct((COLS, 128), jnp.float32),
            jax.ShapeDtypeStruct((COLS, 128), jnp.float32),
        ),
        in_specs=[pl.BlockSpec(memory_space=VMEM)] * 4,
        out_specs=(
            pl.BlockSpec(memory_space=pl.ANY),
            pl.BlockSpec(memory_space=VMEM),
            pl.BlockSpec(memory_space=VMEM),
        ),
        scratch_shapes=[
            VMEM((STEPS + 1, 4, cells_x + 2, cells_y + 2, RHS, 128), jnp.float32),
            VMEM((3 * height, 3 * height), jnp.float32),
            VMEM((count_y, COLS, 128), jnp.float32),
            VMEM((count_x, COLS, 128), jnp.float32),
            dma((STEPS, 2)),
            dma((STEPS, 2)),
            dma((STEPS, 2)),
            dma((STEPS, 2)),
            dma((count_y,)),
            dma((count_y,)),
            dma((count_x,)),
            dma((count_x,)),
            dma((STEPS + 1,)),
        ],
        compiler_params=pltpu.CompilerParams(
            collective_id=0, has_side_effects=True, vmem_limit_bytes=40 * 1024 * 1024
        ),
        name="basis",
    )(
        mask.reshape(RHS * grid_cells, 128),
        forcing.reshape(RHS * 4 * grid_cells, 128),
        flow,
        shear,
    )


def orthonormal_kernel(
    all_cells, cells_y,
    basis_ref, inverse_ref, factor_ref, permute_ref, mix_ref,
    q_ref, r_ref, rms_ref,
):
    @pl.when((pl.program_id(0) == 0) & (pl.program_id(1) == 0))
    def _():
        rows = jnp.dot(
            permute_ref[...], factor_ref[:, 0:COLS],
            precision=HIGHEST, preferred_element_type=jnp.float32,
        )
        factor = jnp.dot(
            rows, mix_ref[...], precision=HIGHEST, preferred_element_type=jnp.float32
        )
        r_ref[...] = factor
        rms_ref[...] = jnp.sqrt(jnp.sum(factor * factor, axis=0, keepdims=True) / all_cells)

    block = jnp.concatenate([basis_ref[0, 0, y] for y in range(cells_y)], axis=1)
    result = jnp.dot(
        inverse_ref[:, 0:COLS], block, precision=HIGHEST, preferred_element_type=jnp.float32
    )
    q_rows = q_ref.reshape(COLS * cells_y, 128)
    for y in range(cells_y):
        for k in range(STEPS):
            q_rows[pl.ds(k * cells_y + y, RHS, stride=STEPS * cells_y), :] = result[
                k * RHS : (k + 1) * RHS, y * 128 : (y + 1) * 128
            ]


def orthonormal(all_cells, basis_rows, inverse, factor):
    fields, cells_x, cells_y, _, _ = basis_rows.shape
    permute, mix = output_constants()
    whole = lambda *shape: pl.BlockSpec(shape, lambda f, x: (0,) * len(shape))
    return pl.pallas_call(
        functools.partial(orthonormal_kernel, all_cells, cells_y),
        grid=(fields, cells_x),
        out_shape=(
            jax.ShapeDtypeStruct((COLS, fields, cells_x, cells_y, 128), jnp.float32),
            jax.ShapeDtypeStruct((COLS, COLS), jnp.float32),
            jax.ShapeDtypeStruct((1, COLS), jnp.float32),
        ),
        in_specs=[
            pl.BlockSpec((1, 1, cells_y, COLS, 128), lambda f, x: (f, x, 0, 0, 0)),
            whole(COLS, 128),
            whole(COLS, 128),
            whole(COLS, COLS),
            whole(COLS, COLS),
        ],
        out_specs=(
            pl.BlockSpec((COLS, 1, 1, cells_y, 128), lambda f, x: (0, f, x, 0, 0)),
            whole(COLS, COLS),
            whole(1, COLS),
        ),
        compiler_params=pltpu.CompilerParams(vmem_limit_bytes=24 * 1024 * 1024),
        name="orthonormal",
    )(basis_rows, inverse, factor, jnp.asarray(permute), jnp.asarray(mix))


def shards(actuator_mask, forcing, base_flow, base_shear):
    _, cells_x, cells_y, cells_z = base_flow.shape
    counts = (lax.axis_size("gx"), lax.axis_size("gy"))
    all_cells = 4.0 * cells_x * counts[0] * cells_y * counts[1] * cells_z
    rows, inverse, factor = basis(actuator_mask, forcing, base_flow, base_shear, counts)
    q_basis, r_factor, rms = orthonormal(all_cells, rows, inverse, factor)
    return (q_basis, r_factor, rms[0])


def solution(mesh):
    return jax.shard_map(
        shards,
        mesh=mesh,
        in_specs=(
            P(None, "gx", "gy", None),
            P(None, None, "gx", "gy", None),
            P(None, "gx", "gy", None),
            P(None, None, "gx", "gy", None),
        ),
        out_specs=(P(None, None, "gx", "gy", None), P(), P()),
        check_vma=False,
    )
```

```python
import functools

import jax
import jax.numpy as jnp
import numpy as np
from jax import lax
from jax.experimental import pallas as pl
from jax.experimental.pallas import tpu as pltpu
from jax.sharding import PartitionSpec as P

S = 8
RHS = 8
STEPS = S + 1
COLS = RHS * STEPS
PAIRS = (STEPS + 1) // 2
PAIR = 48
VMEM = pltpu.VMEM
MESH = pl.DeviceIdType.MESH
HIGHEST = lax.Precision.HIGHEST

viscosity = 0.04
diffusivity = 0.04
coupling = 0.5
spectral_shift = 0.5

SHIFT = -(6.0 * viscosity + spectral_shift)
BACK = 0.2


def change_of_basis():
    hessenberg = np.zeros((STEPS, STEPS))
    for k in range(STEPS):
        hessenberg[k, k] = SHIFT
        if k + 1 < STEPS:
            hessenberg[k + 1, k] = 1.0
        if k > 0:
            hessenberg[k - 1, k] = -BACK
    change = np.zeros((STEPS, STEPS))
    column = np.zeros(STEPS)
    column[0] = 1.0
    for k in range(STEPS):
        change[:, k] = column
        column = hessenberg @ column
    return change


def place(order):
    source, k = divmod(order, STEPS)
    return k * RHS + source


def output_constants():
    change = change_of_basis()
    permute = np.zeros((COLS, COLS), np.float32)
    mix = np.zeros((COLS, COLS), np.float32)
    for i in range(COLS):
        permute[i, place(i)] = 1.0
    for r in range(RHS):
        for a in range(STEPS):
            for b in range(STEPS):
                mix[a * RHS + r, r * STEPS + b] = change[a, b]
    return permute, mix


def split3(value):
    high = value.astype(jnp.bfloat16)
    rest = value - high.astype(jnp.float32)
    middle = rest.astype(jnp.bfloat16)
    low = (rest - middle.astype(jnp.float32)).astype(jnp.bfloat16)
    return high, middle, low


def basis_kernel(
    counts, cells,
    mask_hbm, forcing_hbm, flow_hbm, shear_hbm,
    parts, inverse_ref, factor_ref,
    mask_ref, forcing_ref, flow_ref, shear_ref, fields, gram, one, two,
    send_x, recv_x, send_y, recv_y, send_one, recv_one, send_two, recv_two, load_sem,
):
    count_x, count_y = counts
    cells_x, cells_y = cells
    gx = lax.axis_index("gx")
    gy = lax.axis_index("gy")

    arrays = (
        (forcing_hbm, forcing_ref), (mask_hbm, mask_ref),
        (flow_hbm, flow_ref), (shear_hbm, shear_ref),
    )
    loads = [pltpu.make_async_copy(a, b, load_sem.at[n]) for n, (a, b) in enumerate(arrays)]
    for copy in loads:
        copy.start()
    early, late = loads[:2], loads[2:]

    barrier = pltpu.get_barrier_semaphore()
    for step in range(1, count_x):
        pl.semaphore_signal(
            barrier, inc=1, device_id=(lax.rem(gx + step, count_x), gy), device_id_type=MESH
        )
    for step in range(1, count_y):
        pl.semaphore_signal(
            barrier, inc=1, device_id=(gx, lax.rem(gy + step, count_y)), device_id_type=MESH
        )

    zero = jnp.zeros((8, 128), jnp.float32)
    lane = lax.broadcasted_iota(jnp.int32, (8, 128), 1)
    first_lane, last_lane = lane == 0, lane == 127

    def clear(k, carry):
        @pl.when(gx == 0)
        def _():
            fields[k, :, 0] = jnp.zeros(fields.shape[1:2] + fields.shape[3:], jnp.float32)

        @pl.when(gx == count_x - 1)
        def _():
            fields[k, :, cells_x + 1] = jnp.zeros(
                fields.shape[1:2] + fields.shape[3:], jnp.float32
            )

        @pl.when(gy == 0)
        def _():
            fields[k, :, :, 0] = jnp.zeros(fields.shape[1:3] + fields.shape[4:], jnp.float32)

        @pl.when(gy == count_y - 1)
        def _():
            fields[k, :, :, cells_y + 1] = jnp.zeros(
                fields.shape[1:3] + fields.shape[4:], jnp.float32
            )

        return carry

    lax.fori_loop(1, STEPS, clear, 0)
    fields[0] = jnp.zeros(fields.shape[1:], jnp.float32)

    def start_row(i, carry):
        x, y = i // cells_y, lax.rem(i, cells_y)
        mask = mask_ref[pl.ds(i, RHS, stride=cells_x * cells_y), :].astype(jnp.float32)
        for f in range(4):
            where = f * cells_x * cells_y + i
            value = forcing_ref[pl.ds(where, RHS, stride=4 * cells_x * cells_y), :]
            fields[1, f, x + 1, y + 1] = value * mask
        return carry

    for copy in early:
        copy.wait()
    lax.fori_loop(0, cells_x * cells_y, start_row, 0)
    pl.semaphore_wait(barrier, count_x + count_y - 2)

    def halo(k, axis, up):
        side = 1 if up else 0
        if axis == 0:
            source = cells_x if up else 1
            target = 0 if up else cells_x + 1
            rows = pl.ds(1, cells_y)
            return pltpu.make_async_remote_copy(
                src_ref=fields.at[k, :, source, rows],
                dst_ref=fields.at[k, :, target, rows],
                send_sem=send_x.at[k, side],
                recv_sem=recv_x.at[k, side],
                device_id=(gx + 1 if up else gx - 1, gy),
                device_id_type=MESH,
            )
        source = cells_y if up else 1
        target = 0 if up else cells_y + 1
        rows = pl.ds(1, cells_x)
        return pltpu.make_async_remote_copy(
            src_ref=fields.at[k, :, rows, source],
            dst_ref=fields.at[k, :, rows, target],
            send_sem=send_y.at[k, side],
            recv_sem=recv_y.at[k, side],
            device_id=(gx, gy + 1 if up else gy - 1),
            device_id_type=MESH,
        )

    def at_sides(k, axis, what):
        me, count = (gx, count_x) if axis == 0 else (gy, count_y)
        for up in (True, False):
            sends = me < count - 1 if up else me > 0
            receives = me > 0 if up else me < count - 1

            @pl.when(receives if what == "recv" else sends)
            def _(up=up):
                copy = halo(k, axis, up)
                if what == "start":
                    copy.start()
                elif what == "send":
                    copy.wait_send()
                else:
                    copy.wait_recv()

    def advance(k, x, y):
        def value(f, dx=0, dy=0):
            return fields[k, f, x + 1 + dx, y + 1 + dy]

        centre = [value(f) for f in range(4)]
        plus = [
            [value(f, 1, 0) for f in range(4)],
            [value(f, 0, 1) for f in range(4)],
            [jnp.where(last_lane, zero, pltpu.roll(centre[f], 127, 1)) for f in range(4)],
        ]
        minus = [
            [value(f, -1, 0) for f in range(4)],
            [value(f, 0, -1) for f in range(4)],
            [jnp.where(first_lane, zero, pltpu.roll(centre[f], 1, 1)) for f in range(4)],
        ]
        result = [BACK * fields[k - 1, f, x + 1, y + 1] for f in range(4)]
        for j in range(3):
            half = 0.5 * flow_ref[j, x, pl.ds(y, 1), :]
            ahead = jnp.broadcast_to(viscosity - half, (8, 128))
            behind = jnp.broadcast_to(viscosity + half, (8, 128))
            for i in range(3):
                result[i] = result[i] + ahead * plus[j][i] + behind * minus[j][i]
                shear = jnp.broadcast_to(shear_ref[i, j, x, pl.ds(y, 1), :], (8, 128))
                result[i] = result[i] - shear * centre[j]
            result[j] = result[j] - 0.5 * (plus[j][3] - minus[j][3])
            result[3] = result[3] + diffusivity * (plus[j][3] + minus[j][3])
            result[3] = result[3] - (0.5 * coupling) * (plus[j][j] - minus[j][j])
        for f in range(4):
            fields[k + 1, f, x + 1, y + 1] = result[f]

    def inner_products(pair, i, second=True):
        f, x = i // cells_x, lax.rem(i, cells_x)
        k = 2 * pair + 1
        first = jnp.concatenate([fields[k, f, x + 1, y + 1] for y in range(cells_y)], axis=1)
        if second:
            other = jnp.concatenate(
                [fields[k + 1, f, x + 1, y + 1] for y in range(cells_y)], axis=1
            )
        else:
            other = jnp.zeros_like(first)
        new = jnp.concatenate(split3(jnp.concatenate([first, other], axis=0)), axis=0)
        where = pl.ds(PAIR * pair if isinstance(pair, int) else pl.multiple_of(PAIR * pair, 16), PAIR)
        parts[i, where, :] = new
        gram[pair] += lax.dot_general(
            parts[i], new, (((1,), (1,)), ((), ())), preferred_element_type=jnp.float32
        )

    def section(k):
        def x_faces(y, carry):
            advance(k, 0, y)
            advance(k, cells_x - 1, y)
            return carry

        def y_faces(x, carry):
            advance(k, x, 0)
            advance(k, x, cells_y - 1)
            return carry

        def inside(y, carry):
            for x in range(1, cells_x - 1):
                advance(k, x, y)
            return carry

        at_sides(k, 0, "recv")
        at_sides(k, 1, "recv")
        lax.fori_loop(0, cells_y, x_faces, 0)

        @pl.when(k < S)
        def _():
            at_sides(k + 1, 0, "start")

        lax.fori_loop(1, cells_x - 1, y_faces, 0)

        @pl.when(k < S)
        def _():
            at_sides(k + 1, 1, "start")

        lax.fori_loop(1, cells_y - 1, inside, 0)

    at_sides(1, 0, "start")
    at_sides(1, 1, "start")
    gram[...] = jnp.zeros_like(gram)
    parts[...] = jnp.zeros_like(parts)
    for copy in late:
        copy.wait()
    blocks = 4 * cells_x

    def two_sections(pair, carry):
        def products(i, carry):
            inner_products(pair, i)
            return carry

        section(2 * pair + 1)
        lax.fori_loop(0, blocks // 2, products, 0)
        section(2 * pair + 2)
        lax.fori_loop(blocks // 2, blocks, products, 0)
        return carry

    lax.fori_loop(0, S // 2, two_sections, 0)

    def last_products(i, carry):
        inner_products(S // 2, i, second=False)
        return carry

    lax.fori_loop(0, blocks, last_products, 0)

    pieces = []
    for pair in range(PAIRS):
        block = gram[pair]
        block = block[:, 0:16] + block[:, 16:32] + block[:, 32:48]
        tall = [
            block[PAIR * a : PAIR * a + 16]
            + block[PAIR * a + 16 : PAIR * a + 32]
            + block[PAIR * a + 32 : PAIR * a + 48]
            for a in range(pair + 1)
        ]
        tall = tall + [jnp.zeros((16 * (PAIRS - 1 - pair), 16), jnp.float32)] * (pair + 1 < PAIRS)
        pieces.append(jnp.concatenate(tall, axis=0))
    pieces.append(jnp.zeros((16 * PAIRS, 128 - 16 * PAIRS), jnp.float32))
    own = jnp.concatenate(pieces, axis=1)[0:COLS]

    def exchange(slots, me, count, device, send, recv):
        def copy(step, slot, partner):
            return pltpu.make_async_remote_copy(
                src_ref=slots.at[slot],
                dst_ref=slots.at[slot],
                send_sem=send.at[step],
                recv_sem=recv.at[step],
                device_id=device(partner),
                device_id_type=MESH,
            )

        for step in range(1, count):
            copy(step, me, lax.rem(me + step, count)).start()
        for step in range(1, count):
            source = lax.rem(me + count - step, count)
            copy(step, source, source).wait_recv()
        total = slots[0]
        for slot in range(1, count):
            total = total + slots[slot]
        for step in range(1, count):
            copy(step, me, lax.rem(me + step, count)).wait_send()
        return total

    one[gy] = own
    own = exchange(one, gy, count_y, lambda p: (gx, p), send_one, recv_one)
    two[gx] = own
    matrix = exchange(two, gx, count_x, lambda p: (p, gy), send_two, recv_two)

    rows = lax.broadcasted_iota(jnp.int32, (COLS, 128), 0)
    columns = lax.broadcasted_iota(jnp.int32, (COLS, 128), 1)
    square = jnp.concatenate([matrix, jnp.zeros((128 - COLS, 128), jnp.float32)], axis=0)
    mirror = jnp.transpose(square)[0:COLS]
    matrix = jnp.where(rows // 16 <= columns // 16, matrix, mirror)

    rank = lax.rem(rows, RHS) * STEPS + rows // RHS
    column_rank = lax.rem(columns, RHS) * STEPS + columns // RHS
    inverse = jnp.where(rows == columns, 1.0, 0.0)
    for source in range(RHS):
        places = [k * RHS + source for k in range(STEPS)]
        spread = [jnp.broadcast_to(matrix[:, p : p + 1], (COLS, 128)) for p in places]
        for k, p in enumerate(places):
            order = source * STEPS + k
            row = matrix[p : p + 1, :]
            inverse_row = inverse[p : p + 1, :]
            pivot = spread[k][p : p + 1, :]
            guess = pl.reciprocal(pivot, approx=True)
            guess = guess * (2.0 - pivot * guess)
            over = guess * (2.0 - pivot * guess)
            scale = lax.rsqrt(pivot)
            scale = scale * (1.5 - 0.5 * pivot * scale * scale)
            factor_ref[p : p + 1, :] = jnp.where(
                column_rank[0:1, :] >= order, row * scale, 0.0
            )
            inverse_ref[p : p + 1, :] = inverse_row * scale
            if order + 1 < COLS:
                multiple = jnp.where(rank > order, spread[k], 0.0)
                matrix = matrix - multiple * (row * over)
                inverse = inverse - multiple * (inverse_row * over)
                for l in range(k + 1, STEPS):
                    entry = spread[l][p : p + 1, :] * over
                    spread[l] = spread[l] - multiple * entry
    inverse_ref[COLS:, :] = jnp.zeros((16 * PAIRS - COLS, 128), jnp.float32)

    def finish(k, carry):
        at_sides(k, 0, "send")
        at_sides(k, 1, "send")
        return carry

    lax.fori_loop(1, STEPS, finish, 0)


def basis(mask, forcing, flow, shear, counts):
    _, cells_x, cells_y, _ = flow.shape
    cells = (cells_x, cells_y)
    grid_cells = cells_x * cells_y
    count_x, count_y = counts
    dma = pltpu.SemaphoreType.DMA
    height = 16 * PAIRS
    return pl.pallas_call(
        functools.partial(basis_kernel, counts, cells),
        out_shape=(
            jax.ShapeDtypeStruct((4 * cells_x, PAIR * PAIRS, cells_y * 128), jnp.bfloat16),
            jax.ShapeDtypeStruct((height, 128), jnp.float32),
            jax.ShapeDtypeStruct((COLS, 128), jnp.float32),
        ),
        in_specs=[pl.BlockSpec(memory_space=pltpu.HBM)] * 4,
        out_specs=(pl.BlockSpec(memory_space=VMEM),) * 3,
        scratch_shapes=[
            VMEM((RHS * grid_cells, 128), jnp.int32),
            VMEM((RHS * 4 * grid_cells, 128), jnp.float32),
            VMEM(flow.shape, jnp.float32),
            VMEM(shear.shape, jnp.float32),
            VMEM((STEPS + 1, 4, cells_x + 2, cells_y + 2, RHS, 128), jnp.float32),
            VMEM((PAIRS, PAIR * PAIRS, PAIR), jnp.float32),
            VMEM((count_y, COLS, 128), jnp.float32),
            VMEM((count_x, COLS, 128), jnp.float32),
            dma((STEPS, 2)),
            dma((STEPS, 2)),
            dma((STEPS, 2)),
            dma((STEPS, 2)),
            dma((count_y,)),
            dma((count_y,)),
            dma((count_x,)),
            dma((count_x,)),
            dma((4,)),
        ],
        compiler_params=pltpu.CompilerParams(
            collective_id=0, has_side_effects=True, vmem_limit_bytes=40 * 1024 * 1024
        ),
        name="basis",
    )(
        mask.reshape(RHS * grid_cells, 128),
        forcing.reshape(RHS * 4 * grid_cells, 128),
        flow,
        shear,
    )


def orthonormal_kernel(
    all_cells, cells_y, steps,
    parts_ref, inverse_ref, factor_ref, permute_hbm, mix_hbm,
    q_ref, r_ref, rms_ref,
    left, permute_ref, mix_ref, sem,
):
    step = pl.program_id(0)
    height = 16 * PAIRS
    loads = [
        pltpu.make_async_copy(permute_hbm, permute_ref, sem.at[0]),
        pltpu.make_async_copy(mix_hbm, mix_ref, sem.at[1]),
    ]

    @pl.when(step == 0)
    def _():
        for copy in loads:
            copy.start()
        column = lax.broadcasted_iota(jnp.int32, (height, PAIR * PAIRS), 1)
        row = lax.broadcasted_iota(jnp.int32, (height, PAIR * PAIRS), 0)
        spread = jnp.where(
            row == 16 * (column // PAIR) + lax.rem(column, 16), 1.0, 0.0
        ).astype(jnp.bfloat16)
        high, middle, _ = split3(inverse_ref[:, 0:height])
        both = jnp.concatenate([high, middle], axis=0)
        left[...] = jnp.dot(both, spread, preferred_element_type=jnp.float32).astype(jnp.bfloat16)

    result = jnp.dot(left[...], parts_ref[0], preferred_element_type=jnp.float32)
    result = result[0:COLS] + result[height : height + COLS]
    q_rows = q_ref.reshape(COLS * cells_y, 128)
    for y in range(cells_y):
        for k in range(STEPS):
            q_rows[pl.ds(k * cells_y + y, RHS, stride=STEPS * cells_y), :] = result[
                k * RHS : (k + 1) * RHS, y * 128 : (y + 1) * 128
            ]

    @pl.when(step == steps - 1)
    def _():
        for copy in loads:
            copy.wait()
        rows = jnp.dot(
            permute_ref[...], factor_ref[:, 0:COLS],
            precision=HIGHEST, preferred_element_type=jnp.float32,
        )
        factor = jnp.dot(
            rows, mix_ref[...], precision=HIGHEST, preferred_element_type=jnp.float32
        )
        r_ref[...] = factor
        rms_ref[...] = jnp.sqrt(jnp.sum(factor * factor, axis=0, keepdims=True) / all_cells)


def orthonormal(all_cells, cells, parts, inverse, factor):
    cells_x, cells_y = cells
    steps, depth, width = parts.shape
    height = 16 * PAIRS
    permute, mix = output_constants()
    whole = lambda *shape: pl.BlockSpec(shape, lambda i: (0,) * len(shape))
    return pl.pallas_call(
        functools.partial(orthonormal_kernel, all_cells, cells_y, steps),
        grid=(steps,),
        out_shape=(
            jax.ShapeDtypeStruct((COLS, steps, cells_y, 128), jnp.float32),
            jax.ShapeDtypeStruct((COLS, COLS), jnp.float32),
            jax.ShapeDtypeStruct((1, COLS), jnp.float32),
        ),
        in_specs=[
            pl.BlockSpec((1, depth, width), lambda i: (i, 0, 0)),
            whole(height, 128),
            whole(COLS, 128),
            pl.BlockSpec(memory_space=pltpu.HBM),
            pl.BlockSpec(memory_space=pltpu.HBM),
        ],
        out_specs=(
            pl.BlockSpec((COLS, 1, cells_y, 128), lambda i: (0, i, 0, 0)),
            whole(COLS, COLS),
            whole(1, COLS),
        ),
        scratch_shapes=[
            VMEM((2 * height, depth), jnp.bfloat16),
            VMEM((COLS, COLS), jnp.float32),
            VMEM((COLS, COLS), jnp.float32),
            pltpu.SemaphoreType.DMA((2,)),
        ],
        compiler_params=pltpu.CompilerParams(vmem_limit_bytes=24 * 1024 * 1024),
        name="orthonormal",
    )(parts, inverse, factor, jnp.asarray(permute), jnp.asarray(mix))


def shards(actuator_mask, forcing, base_flow, base_shear):
    _, cells_x, cells_y, cells_z = base_flow.shape
    counts = (lax.axis_size("gx"), lax.axis_size("gy"))
    all_cells = 4.0 * cells_x * counts[0] * cells_y * counts[1] * cells_z
    rows, inverse, factor = basis(actuator_mask, forcing, base_flow, base_shear, counts)
    q_basis, r_factor, rms = orthonormal(all_cells, (cells_x, cells_y), rows, inverse, factor)
    return (q_basis.reshape(COLS, 4, cells_x, cells_y, cells_z), r_factor, rms[0])


def solution(mesh):
    return jax.shard_map(
        shards,
        mesh=mesh,
        in_specs=(
            P(None, "gx", "gy", None),
            P(None, None, "gx", "gy", None),
            P(None, "gx", "gy", None),
            P(None, None, "gx", "gy", None),
        ),
        out_specs=(P(None, None, "gx", "gy", None), P(), P()),
        check_vma=False,
    )
```

```python
import functools

import jax
import jax.numpy as jnp
import numpy as np
from jax import lax
from jax.experimental import pallas as pl
from jax.experimental.pallas import tpu as pltpu
from jax.sharding import PartitionSpec as P

S = 8
RHS = 8
STEPS = S + 1
COLS = RHS * STEPS
PAIRS = (STEPS + 1) // 2
PAIR = 48
PIECES = 4
VMEM = pltpu.VMEM
MESH = pl.DeviceIdType.MESH
HIGHEST = lax.Precision.HIGHEST

viscosity = 0.04
diffusivity = 0.04
coupling = 0.5
spectral_shift = 0.5

SHIFT = -(6.0 * viscosity + spectral_shift)
BACK = 0.2


def change_of_basis():
    hessenberg = np.zeros((STEPS, STEPS))
    for k in range(STEPS):
        hessenberg[k, k] = SHIFT
        if k + 1 < STEPS:
            hessenberg[k + 1, k] = 1.0
        if k > 0:
            hessenberg[k - 1, k] = -BACK
    change = np.zeros((STEPS, STEPS))
    column = np.zeros(STEPS)
    column[0] = 1.0
    for k in range(STEPS):
        change[:, k] = column
        column = hessenberg @ column
    return change


def place(order):
    source, k = divmod(order, STEPS)
    return k * RHS + source


def permutation(height, width):
    rows = lax.broadcasted_iota(jnp.int32, (height, width), 0)
    columns = lax.broadcasted_iota(jnp.int32, (height, width), 1)
    places = lax.rem(rows, STEPS) * RHS + rows // STEPS
    return jnp.where((places == columns) & (rows < COLS), 1.0, 0.0)


def mixing():
    change = change_of_basis()
    rows = lax.broadcasted_iota(jnp.int32, (COLS, COLS), 0)
    columns = lax.broadcasted_iota(jnp.int32, (COLS, COLS), 1)
    degree = jnp.where(
        lax.rem(rows, RHS) == columns // STEPS, STEPS * (rows // RHS) + lax.rem(columns, STEPS), -1
    )
    mix = jnp.zeros((COLS, COLS), jnp.float32)
    for a in range(STEPS):
        for b in range(a, STEPS):
            mix = jnp.where(degree == STEPS * a + b, float(change[a, b]), mix)
    return mix


def split3(value):
    high = value.astype(jnp.bfloat16)
    rest = value - high.astype(jnp.float32)
    middle = rest.astype(jnp.bfloat16)
    low = (rest - middle.astype(jnp.float32)).astype(jnp.bfloat16)
    return high, middle, low


def basis_kernel(
    counts, cells,
    mask_hbm, forcing_hbm, flow_hbm, shear_hbm,
    parts_hbm, inverse_ref, factor_ref,
    mask_ref, forcing_ref, flow_ref, shear_ref, parts, fields, gram, one, two,
    send_x, recv_x, send_y, recv_y, send_one, recv_one, send_two, recv_two, load_sem, save_sem,
):
    count_x, count_y = counts
    cells_x, cells_y = cells
    depth = cells_y // PIECES
    gx = lax.axis_index("gx")
    gy = lax.axis_index("gy")

    arrays = (
        (forcing_hbm, forcing_ref), (mask_hbm, mask_ref),
        (flow_hbm, flow_ref), (shear_hbm, shear_ref),
    )
    loads = [pltpu.make_async_copy(a, b, load_sem.at[n]) for n, (a, b) in enumerate(arrays)]
    for copy in loads:
        copy.start()
    early, late = loads[:2], loads[2:]

    barrier = pltpu.get_barrier_semaphore()
    for step in range(1, count_x):
        pl.semaphore_signal(
            barrier, inc=1, device_id=(lax.rem(gx + step, count_x), gy), device_id_type=MESH
        )
    for step in range(1, count_y):
        pl.semaphore_signal(
            barrier, inc=1, device_id=(gx, lax.rem(gy + step, count_y)), device_id_type=MESH
        )

    zero = jnp.zeros((8, 128), jnp.float32)
    lane = lax.broadcasted_iota(jnp.int32, (8, 128), 1)
    first_lane, last_lane = lane == 0, lane == 127

    def clear(k, carry):
        @pl.when(gx == 0)
        def _():
            fields[k, :, 0] = jnp.zeros(fields.shape[1:2] + fields.shape[3:], jnp.float32)

        @pl.when(gx == count_x - 1)
        def _():
            fields[k, :, cells_x + 1] = jnp.zeros(
                fields.shape[1:2] + fields.shape[3:], jnp.float32
            )

        @pl.when(gy == 0)
        def _():
            fields[k, :, :, 0] = jnp.zeros(fields.shape[1:3] + fields.shape[4:], jnp.float32)

        @pl.when(gy == count_y - 1)
        def _():
            fields[k, :, :, cells_y + 1] = jnp.zeros(
                fields.shape[1:3] + fields.shape[4:], jnp.float32
            )

        return carry

    lax.fori_loop(1, STEPS, clear, 0)
    fields[0] = jnp.zeros(fields.shape[1:], jnp.float32)

    def start_row(i, carry):
        x, y = i // cells_y, lax.rem(i, cells_y)
        mask = mask_ref[pl.ds(i, RHS, stride=cells_x * cells_y), :].astype(jnp.float32)
        for f in range(4):
            where = f * cells_x * cells_y + i
            value = forcing_ref[pl.ds(where, RHS, stride=4 * cells_x * cells_y), :]
            fields[1, f, x + 1, y + 1] = value * mask
        return carry

    for copy in early:
        copy.wait()
    lax.fori_loop(0, cells_x * cells_y, start_row, 0)
    pl.semaphore_wait(barrier, count_x + count_y - 2)

    def halo(k, axis, up, piece):
        side = 1 if up else 0
        if axis == 0:
            source = cells_x if up else 1
            target = 0 if up else cells_x + 1
            rows = pl.ds(1 + piece * depth, depth)
            return pltpu.make_async_remote_copy(
                src_ref=fields.at[k, :, source, rows],
                dst_ref=fields.at[k, :, target, rows],
                send_sem=send_x.at[k, side, piece],
                recv_sem=recv_x.at[k, side, piece],
                device_id=(gx + 1 if up else gx - 1, gy),
                device_id_type=MESH,
            )
        source = cells_y if up else 1
        target = 0 if up else cells_y + 1
        rows = pl.ds(1, cells_x)
        return pltpu.make_async_remote_copy(
            src_ref=fields.at[k, :, rows, source],
            dst_ref=fields.at[k, :, rows, target],
            send_sem=send_y.at[k, side],
            recv_sem=recv_y.at[k, side],
            device_id=(gx, gy + 1 if up else gy - 1),
            device_id_type=MESH,
        )

    def at_sides(k, axis, what, piece=0):
        me, count = (gx, count_x) if axis == 0 else (gy, count_y)
        for up in (True, False):
            sends = me < count - 1 if up else me > 0
            receives = me > 0 if up else me < count - 1

            @pl.when(receives if what == "recv" else sends)
            def _(up=up):
                copy = halo(k, axis, up, piece)
                if what == "start":
                    copy.start()
                elif what == "send":
                    copy.wait_send()
                else:
                    copy.wait_recv()

    def advance(k, x, y):
        def value(f, dx=0, dy=0):
            return fields[k, f, x + 1 + dx, y + 1 + dy]

        centre = [value(f) for f in range(4)]
        plus = [
            [value(f, 1, 0) for f in range(4)],
            [value(f, 0, 1) for f in range(4)],
            [jnp.where(last_lane, zero, pltpu.roll(centre[f], 127, 1)) for f in range(4)],
        ]
        minus = [
            [value(f, -1, 0) for f in range(4)],
            [value(f, 0, -1) for f in range(4)],
            [jnp.where(first_lane, zero, pltpu.roll(centre[f], 1, 1)) for f in range(4)],
        ]
        result = [BACK * fields[k - 1, f, x + 1, y + 1] for f in range(4)]
        for j in range(3):
            half = 0.5 * flow_ref[j, x, pl.ds(y, 1), :]
            ahead = jnp.broadcast_to(viscosity - half, (8, 128))
            behind = jnp.broadcast_to(viscosity + half, (8, 128))
            for i in range(3):
                result[i] = result[i] + ahead * plus[j][i] + behind * minus[j][i]
                shear = jnp.broadcast_to(shear_ref[i, j, x, pl.ds(y, 1), :], (8, 128))
                result[i] = result[i] - shear * centre[j]
            result[j] = result[j] - 0.5 * (plus[j][3] - minus[j][3])
            result[3] = result[3] + diffusivity * (plus[j][3] + minus[j][3])
            result[3] = result[3] - (0.5 * coupling) * (plus[j][j] - minus[j][j])
        for f in range(4):
            fields[k + 1, f, x + 1, y + 1] = result[f]

    def inner_products(pair, i, second=True):
        f, x = i // cells_x, lax.rem(i, cells_x)
        k = 2 * pair + 1
        first = jnp.concatenate([fields[k, f, x + 1, y + 1] for y in range(cells_y)], axis=1)
        if second:
            other = jnp.concatenate(
                [fields[k + 1, f, x + 1, y + 1] for y in range(cells_y)], axis=1
            )
        else:
            other = jnp.zeros_like(first)
        new = jnp.concatenate(split3(jnp.concatenate([first, other], axis=0)), axis=0)
        parts[i, PAIR * pair : PAIR * (pair + 1), :] = new
        below = slice(0, PAIR * (pair + 1))
        gram[pair, below] += lax.dot_general(
            parts[i, below], new, (((1,), (1,)), ((), ())), preferred_element_type=jnp.float32
        )

    def section(k):
        def y_faces(x, carry):
            advance(k, x, 0)
            advance(k, x, cells_y - 1)
            return carry

        def inside(y, carry):
            for x in range(1, cells_x - 1):
                advance(k, x, y)
            return carry

        def piece_of_faces(piece, carry):
            at_sides(k, 0, "recv", piece)
            for y in range(depth):
                advance(k, 0, piece * depth + y)
                advance(k, cells_x - 1, piece * depth + y)

            if k < S:
                at_sides(k + 1, 0, "start", piece)

            return carry

        at_sides(k, 1, "recv")
        lax.fori_loop(0, PIECES, piece_of_faces, 0)
        lax.fori_loop(1, cells_x - 1, y_faces, 0)

        if k < S:
            at_sides(k + 1, 1, "start")

        lax.fori_loop(1, cells_y - 1, inside, 0)

    for piece in range(PIECES):
        at_sides(1, 0, "start", piece)
    at_sides(1, 1, "start")
    gram[...] = jnp.zeros_like(gram)
    for copy in late:
        copy.wait()
    blocks = 4 * cells_x

    def two_sections(pair):
        def products(i, carry):
            inner_products(pair, i)
            return carry

        section(2 * pair + 1)
        lax.fori_loop(0, blocks // 2, products, 0)
        section(2 * pair + 2)
        lax.fori_loop(blocks // 2, blocks, products, 0)

    for pair in range(S // 2):
        two_sections(pair)

    def last_products(i, carry):
        inner_products(S // 2, i, second=False)
        return carry

    lax.fori_loop(0, blocks, last_products, 0)
    save = pltpu.make_async_copy(parts, parts_hbm, save_sem)
    save.start()

    pieces = []
    for pair in range(PAIRS):
        block = gram[pair]
        block = block[:, 0:16] + block[:, 16:32] + block[:, 32:48]
        tall = [
            block[PAIR * a : PAIR * a + 16]
            + block[PAIR * a + 16 : PAIR * a + 32]
            + block[PAIR * a + 32 : PAIR * a + 48]
            for a in range(pair + 1)
        ]
        tall = tall + [jnp.zeros((16 * (PAIRS - 1 - pair), 16), jnp.float32)] * (pair + 1 < PAIRS)
        pieces.append(jnp.concatenate(tall, axis=0))
    pieces.append(jnp.zeros((16 * PAIRS, 128 - 16 * PAIRS), jnp.float32))
    own = jnp.concatenate(pieces, axis=1)[0:COLS]

    def exchange(slots, me, count, device, send, recv):
        def copy(step, slot, partner):
            return pltpu.make_async_remote_copy(
                src_ref=slots.at[slot],
                dst_ref=slots.at[slot],
                send_sem=send.at[step],
                recv_sem=recv.at[step],
                device_id=device(partner),
                device_id_type=MESH,
            )

        for step in range(1, count):
            copy(step, me, lax.rem(me + step, count)).start()
        for step in range(1, count):
            source = lax.rem(me + count - step, count)
            copy(step, source, source).wait_recv()
        total = slots[0]
        for slot in range(1, count):
            total = total + slots[slot]
        for step in range(1, count):
            copy(step, me, lax.rem(me + step, count)).wait_send()
        return total

    one[gy] = own
    own = exchange(one, gy, count_y, lambda p: (gx, p), send_one, recv_one)
    two[gx] = own
    matrix = exchange(two, gx, count_x, lambda p: (p, gy), send_two, recv_two)

    rows = lax.broadcasted_iota(jnp.int32, (COLS, 128), 0)
    columns = lax.broadcasted_iota(jnp.int32, (COLS, 128), 1)
    square = jnp.concatenate([matrix, jnp.zeros((128 - COLS, 128), jnp.float32)], axis=0)
    mirror = jnp.transpose(square)[0:COLS]
    matrix = jnp.where(rows // 16 <= columns // 16, matrix, mirror)

    rank = lax.rem(rows, RHS) * STEPS + rows // RHS
    column_rank = lax.rem(columns, RHS) * STEPS + columns // RHS
    inverse = jnp.where(rows == columns, 1.0, 0.0)
    for source in range(RHS):
        places = [k * RHS + source for k in range(STEPS)]
        spread = [jnp.broadcast_to(matrix[:, p : p + 1], (COLS, 128)) for p in places]
        for k, p in enumerate(places):
            order = source * STEPS + k
            row = matrix[p : p + 1, :]
            inverse_row = inverse[p : p + 1, :]
            pivot = spread[k][p : p + 1, :]
            guess = pl.reciprocal(pivot, approx=True)
            guess = guess * (2.0 - pivot * guess)
            over = guess * (2.0 - pivot * guess)
            scale = lax.rsqrt(pivot)
            scale = scale * (1.5 - 0.5 * pivot * scale * scale)
            factor_ref[p : p + 1, :] = jnp.where(
                column_rank[0:1, :] >= order, row * scale, 0.0
            )
            inverse_ref[p : p + 1, :] = inverse_row * scale
            if order + 1 < COLS:
                multiple = jnp.where(rank > order, spread[k], 0.0)
                matrix = matrix - multiple * (row * over)
                inverse = inverse - multiple * (inverse_row * over)
                for l in range(k + 1, STEPS):
                    entry = spread[l][p : p + 1, :] * over
                    spread[l] = spread[l] - multiple * entry
    inverse_ref[COLS:, :] = jnp.zeros((16 * PAIRS - COLS, 128), jnp.float32)

    def finish(k, carry):
        for piece in range(PIECES):
            at_sides(k, 0, "send", piece)
        at_sides(k, 1, "send")
        return carry

    lax.fori_loop(1, STEPS, finish, 0)
    save.wait()


def basis(mask, forcing, flow, shear, counts):
    _, cells_x, cells_y, _ = flow.shape
    cells = (cells_x, cells_y)
    grid_cells = cells_x * cells_y
    count_x, count_y = counts
    dma = pltpu.SemaphoreType.DMA
    height = 16 * PAIRS
    return pl.pallas_call(
        functools.partial(basis_kernel, counts, cells),
        out_shape=(
            jax.ShapeDtypeStruct((4 * cells_x, PAIR * PAIRS, cells_y * 128), jnp.bfloat16),
            jax.ShapeDtypeStruct((height, 128), jnp.float32),
            jax.ShapeDtypeStruct((COLS, 128), jnp.float32),
        ),
        in_specs=[pl.BlockSpec(memory_space=pltpu.HBM)] * 4,
        out_specs=(
            pl.BlockSpec(memory_space=pltpu.HBM),
            pl.BlockSpec(memory_space=VMEM),
            pl.BlockSpec(memory_space=VMEM),
        ),
        scratch_shapes=[
            VMEM((RHS * grid_cells, 128), jnp.int32),
            VMEM((RHS * 4 * grid_cells, 128), jnp.float32),
            VMEM(flow.shape, jnp.float32),
            VMEM(shear.shape, jnp.float32),
            VMEM((4 * cells_x, PAIR * PAIRS, cells_y * 128), jnp.bfloat16),
            VMEM((STEPS + 1, 4, cells_x + 2, cells_y + 2, RHS, 128), jnp.float32),
            VMEM((PAIRS, PAIR * PAIRS, PAIR), jnp.float32),
            VMEM((count_y, COLS, 128), jnp.float32),
            VMEM((count_x, COLS, 128), jnp.float32),
            dma((STEPS, 2, PIECES)),
            dma((STEPS, 2, PIECES)),
            dma((STEPS, 2)),
            dma((STEPS, 2)),
            dma((count_y,)),
            dma((count_y,)),
            dma((count_x,)),
            dma((count_x,)),
            dma((4,)),
            dma,
        ],
        compiler_params=pltpu.CompilerParams(
            collective_id=0, has_side_effects=True, vmem_limit_bytes=55 * 1024 * 1024
        ),
        name="basis",
    )(
        mask.reshape(RHS * grid_cells, 128),
        forcing.reshape(RHS * 4 * grid_cells, 128),
        flow,
        shear,
    )


def orthonormal_kernel(
    all_cells, cells_y, steps,
    parts_ref, inverse_ref, factor_ref,
    q_ref, r_ref, rms_ref,
    left,
):
    step = pl.program_id(0)
    height = 16 * PAIRS

    @pl.when(step == 0)
    def _():
        column = lax.broadcasted_iota(jnp.int32, (height, PAIR * PAIRS), 1)
        row = lax.broadcasted_iota(jnp.int32, (height, PAIR * PAIRS), 0)
        spread = jnp.where(
            row == 16 * (column // PAIR) + lax.rem(column, 16), 1.0, 0.0
        ).astype(jnp.bfloat16)
        high, middle, _ = split3(inverse_ref[:, 0:height])
        order = permutation(height, height).astype(jnp.bfloat16)
        both = jnp.concatenate(
            [
                jnp.dot(order, part, preferred_element_type=jnp.float32).astype(jnp.bfloat16)
                for part in (high, middle)
            ],
            axis=0,
        )
        left[...] = jnp.dot(both, spread, preferred_element_type=jnp.float32).astype(jnp.bfloat16)

    result = jnp.dot(left[...], parts_ref[0], preferred_element_type=jnp.float32)
    result = result[0:COLS] + result[height : height + COLS]
    planes = [result[:, y * 128 : (y + 1) * 128] for y in range(cells_y)]
    q_ref[:, 0] = jnp.swapaxes(jnp.stack(planes, axis=0), 0, 1)

    @pl.when(step == steps - 1)
    def _():
        rows = jnp.dot(
            permutation(COLS, COLS), factor_ref[:, 0:COLS],
            precision=HIGHEST, preferred_element_type=jnp.float32,
        )
        factor = jnp.dot(
            rows, mixing(), precision=HIGHEST, preferred_element_type=jnp.float32
        )
        r_ref[...] = factor
        rms_ref[...] = jnp.sqrt(jnp.sum(factor * factor, axis=0, keepdims=True) / all_cells)


def orthonormal(all_cells, cells, parts, inverse, factor):
    cells_x, cells_y = cells
    steps, depth, width = parts.shape
    height = 16 * PAIRS
    whole = lambda *shape: pl.BlockSpec(shape, lambda i: (0,) * len(shape))
    return pl.pallas_call(
        functools.partial(orthonormal_kernel, all_cells, cells_y, steps),
        grid=(steps,),
        out_shape=(
            jax.ShapeDtypeStruct((COLS, steps, cells_y, 128), jnp.float32),
            jax.ShapeDtypeStruct((COLS, COLS), jnp.float32),
            jax.ShapeDtypeStruct((1, COLS), jnp.float32),
        ),
        in_specs=[
            pl.BlockSpec((1, depth, width), lambda i: (i, 0, 0)),
            whole(height, 128),
            whole(COLS, 128),
        ],
        out_specs=(
            pl.BlockSpec((COLS, 1, cells_y, 128), lambda i: (0, i, 0, 0)),
            whole(COLS, COLS),
            whole(1, COLS),
        ),
        scratch_shapes=[
            VMEM((2 * height, depth), jnp.bfloat16),
        ],
        compiler_params=pltpu.CompilerParams(vmem_limit_bytes=55 * 1024 * 1024),
        name="orthonormal",
    )(parts, inverse, factor)


def shards(actuator_mask, forcing, base_flow, base_shear):
    _, cells_x, cells_y, cells_z = base_flow.shape
    counts = (lax.axis_size("gx"), lax.axis_size("gy"))
    all_cells = 4.0 * cells_x * counts[0] * cells_y * counts[1] * cells_z
    rows, inverse, factor = basis(actuator_mask, forcing, base_flow, base_shear, counts)
    q_basis, r_factor, rms = orthonormal(all_cells, (cells_x, cells_y), rows, inverse, factor)
    return (q_basis.reshape(COLS, 4, cells_x, cells_y, cells_z), r_factor, rms[0])


def solution(mesh):
    return jax.shard_map(
        shards,
        mesh=mesh,
        in_specs=(
            P(None, "gx", "gy", None),
            P(None, None, "gx", "gy", None),
            P(None, "gx", "gy", None),
            P(None, None, "gx", "gy", None),
        ),
        out_specs=(P(None, None, "gx", "gy", None), P(), P()),
        check_vma=False,
    )
```

```python
import functools

import jax
import jax.numpy as jnp
import numpy as np
from jax import lax
from jax.experimental import pallas as pl
from jax.experimental.pallas import tpu as pltpu
from jax.sharding import PartitionSpec as P

S = 8
RHS = 8
STEPS = S + 1
COLS = RHS * STEPS
PAIRS = (STEPS + 1) // 2
PAIR = 32
PIECES = 4
WIDTH = 128 * (-(-8 * PAIRS * (PAIRS + 1) // 128))
VMEM = pltpu.VMEM
MESH = pl.DeviceIdType.MESH
HIGHEST = lax.Precision.HIGHEST

viscosity = 0.04
diffusivity = 0.04
coupling = 0.5
spectral_shift = 0.5

SHIFT = -(6.0 * viscosity + spectral_shift)
BACK = 0.2


def change_of_basis():
    hessenberg = np.zeros((STEPS, STEPS))
    for k in range(STEPS):
        hessenberg[k, k] = SHIFT
        if k + 1 < STEPS:
            hessenberg[k + 1, k] = 1.0
        if k > 0:
            hessenberg[k - 1, k] = -BACK
    change = np.zeros((STEPS, STEPS))
    column = np.zeros(STEPS)
    column[0] = 1.0
    for k in range(STEPS):
        change[:, k] = column
        column = hessenberg @ column
    return change


def place(order):
    source, k = divmod(order, STEPS)
    return k * RHS + source


def permutation(height, width):
    rows = lax.broadcasted_iota(jnp.int32, (height, width), 0)
    columns = lax.broadcasted_iota(jnp.int32, (height, width), 1)
    places = lax.rem(rows, STEPS) * RHS + rows // STEPS
    return jnp.where((places == columns) & (rows < COLS), 1.0, 0.0)


def mixing():
    change = change_of_basis()
    rows = lax.broadcasted_iota(jnp.int32, (COLS, COLS), 0)
    columns = lax.broadcasted_iota(jnp.int32, (COLS, COLS), 1)
    degree = jnp.where(
        lax.rem(rows, RHS) == columns // STEPS, STEPS * (rows // RHS) + lax.rem(columns, STEPS), -1
    )
    mix = jnp.zeros((COLS, COLS), jnp.float32)
    for a in range(STEPS):
        for b in range(a, STEPS):
            mix = jnp.where(degree == STEPS * a + b, float(change[a, b]), mix)
    return mix


def split2(value):
    high = value.astype(jnp.bfloat16)
    return high, (value - high.astype(jnp.float32)).astype(jnp.bfloat16)


def basis_kernel(
    counts, cells,
    mask_hbm, forcing_hbm, flow_hbm, shear_hbm,
    parts_hbm, inverse_ref, factor_ref,
    mask_ref, forcing_ref, flow_ref, shear_ref, parts, fields, gram, one, two,
    send_x, recv_x, send_y, recv_y, send_one, recv_one, send_two, recv_two, load_sem, save_sem,
):
    count_x, count_y = counts
    cells_x, cells_y = cells
    depth = cells_y // PIECES
    gx = lax.axis_index("gx")
    gy = lax.axis_index("gy")

    arrays = (
        (forcing_hbm, forcing_ref), (mask_hbm, mask_ref),
        (flow_hbm, flow_ref), (shear_hbm, shear_ref),
    )
    loads = [pltpu.make_async_copy(a, b, load_sem.at[n]) for n, (a, b) in enumerate(arrays)]
    for copy in loads:
        copy.start()
    early, late = loads[:2], loads[2:]

    barrier = pltpu.get_barrier_semaphore()
    for step in range(1, count_x):
        pl.semaphore_signal(
            barrier, inc=1, device_id=(lax.rem(gx + step, count_x), gy), device_id_type=MESH
        )
    for step in range(1, count_y):
        pl.semaphore_signal(
            barrier, inc=1, device_id=(gx, lax.rem(gy + step, count_y)), device_id_type=MESH
        )

    zero = jnp.zeros((8, 128), jnp.float32)
    lane = lax.broadcasted_iota(jnp.int32, (8, 128), 1)
    first_lane, last_lane = lane == 0, lane == 127

    def clear(k, carry):
        @pl.when(gx == 0)
        def _():
            fields[k, :, 0] = jnp.zeros(fields.shape[1:2] + fields.shape[3:], jnp.float32)

        @pl.when(gx == count_x - 1)
        def _():
            fields[k, :, cells_x + 1] = jnp.zeros(
                fields.shape[1:2] + fields.shape[3:], jnp.float32
            )

        @pl.when(gy == 0)
        def _():
            fields[k, :, :, 0] = jnp.zeros(fields.shape[1:3] + fields.shape[4:], jnp.float32)

        @pl.when(gy == count_y - 1)
        def _():
            fields[k, :, :, cells_y + 1] = jnp.zeros(
                fields.shape[1:3] + fields.shape[4:], jnp.float32
            )

        return carry

    lax.fori_loop(1, STEPS, clear, 0)
    fields[0] = jnp.zeros(fields.shape[1:], jnp.float32)

    def start_row(i, carry):
        x, y = i // cells_y, lax.rem(i, cells_y)
        mask = mask_ref[pl.ds(i, RHS, stride=cells_x * cells_y), :].astype(jnp.float32)
        for f in range(4):
            where = f * cells_x * cells_y + i
            value = forcing_ref[pl.ds(where, RHS, stride=4 * cells_x * cells_y), :]
            fields[1, f, x + 1, y + 1] = value * mask
        return carry

    for copy in early:
        copy.wait()
    lax.fori_loop(0, cells_x * cells_y, start_row, 0)
    pl.semaphore_wait(barrier, count_x + count_y - 2)

    def halo(k, axis, up, piece):
        side = 1 if up else 0
        if axis == 0:
            source = cells_x if up else 1
            target = 0 if up else cells_x + 1
            rows = pl.ds(1 + piece * depth, depth)
            return pltpu.make_async_remote_copy(
                src_ref=fields.at[k, :, source, rows],
                dst_ref=fields.at[k, :, target, rows],
                send_sem=send_x.at[k, side, piece],
                recv_sem=recv_x.at[k, side, piece],
                device_id=(gx + 1 if up else gx - 1, gy),
                device_id_type=MESH,
            )
        source = cells_y if up else 1
        target = 0 if up else cells_y + 1
        rows = pl.ds(1, cells_x)
        return pltpu.make_async_remote_copy(
            src_ref=fields.at[k, :, rows, source],
            dst_ref=fields.at[k, :, rows, target],
            send_sem=send_y.at[k, side],
            recv_sem=recv_y.at[k, side],
            device_id=(gx, gy + 1 if up else gy - 1),
            device_id_type=MESH,
        )

    def at_sides(k, axis, what, piece=0):
        me, count = (gx, count_x) if axis == 0 else (gy, count_y)
        for up in (True, False):
            sends = me < count - 1 if up else me > 0
            receives = me > 0 if up else me < count - 1

            @pl.when(receives if what == "recv" else sends)
            def _(up=up):
                copy = halo(k, axis, up, piece)
                if what == "start":
                    copy.start()
                elif what == "send":
                    copy.wait_send()
                else:
                    copy.wait_recv()

    def advance(k, x, y):
        def value(f, dx=0, dy=0):
            return fields[k, f, x + 1 + dx, y + 1 + dy]

        centre = [value(f) for f in range(4)]
        plus = [
            [value(f, 1, 0) for f in range(4)],
            [value(f, 0, 1) for f in range(4)],
            [jnp.where(last_lane, zero, pltpu.roll(centre[f], 127, 1)) for f in range(4)],
        ]
        minus = [
            [value(f, -1, 0) for f in range(4)],
            [value(f, 0, -1) for f in range(4)],
            [jnp.where(first_lane, zero, pltpu.roll(centre[f], 1, 1)) for f in range(4)],
        ]
        result = [BACK * fields[k - 1, f, x + 1, y + 1] for f in range(4)]
        for j in range(3):
            half = 0.5 * flow_ref[j, x, pl.ds(y, 1), :]
            ahead = jnp.broadcast_to(viscosity - half, (8, 128))
            behind = jnp.broadcast_to(viscosity + half, (8, 128))
            for i in range(3):
                result[i] = result[i] + ahead * plus[j][i] + behind * minus[j][i]
                shear = jnp.broadcast_to(shear_ref[i, j, x, pl.ds(y, 1), :], (8, 128))
                result[i] = result[i] - shear * centre[j]
            result[j] = result[j] - 0.5 * (plus[j][3] - minus[j][3])
            result[3] = result[3] + diffusivity * (plus[j][3] + minus[j][3])
            result[3] = result[3] - (0.5 * coupling) * (plus[j][j] - minus[j][j])
        for f in range(4):
            fields[k + 1, f, x + 1, y + 1] = result[f]

    def inner_products(pair, i, second=True):
        f, x = i // cells_x, lax.rem(i, cells_x)
        k = 2 * pair + 1
        first = jnp.concatenate([fields[k, f, x + 1, y + 1] for y in range(cells_y)], axis=1)
        if second:
            other = jnp.concatenate(
                [fields[k + 1, f, x + 1, y + 1] for y in range(cells_y)], axis=1
            )
        else:
            other = jnp.zeros_like(first)
        new = jnp.concatenate(split2(jnp.concatenate([first, other], axis=0)), axis=0)
        parts[i, PAIR * pair : PAIR * (pair + 1), :] = new
        below = slice(0, PAIR * (pair + 1))
        gram[pair, below] += lax.dot_general(
            parts[i, below], new, (((1,), (1,)), ((), ())), preferred_element_type=jnp.float32
        )

    def section(k):
        def y_faces(x, carry):
            advance(k, x, 0)
            advance(k, x, cells_y - 1)
            return carry

        def inside(y, carry):
            for x in range(1, cells_x - 1):
                advance(k, x, y)
            return carry

        def piece_of_faces(piece, carry):
            at_sides(k, 0, "recv", piece)
            for y in range(depth):
                advance(k, 0, piece * depth + y)
                advance(k, cells_x - 1, piece * depth + y)

            if k < S:
                at_sides(k + 1, 0, "start", piece)

            return carry

        at_sides(k, 1, "recv")
        lax.fori_loop(0, PIECES, piece_of_faces, 0)
        lax.fori_loop(1, cells_x - 1, y_faces, 0)

        if k < S:
            at_sides(k + 1, 1, "start")

        lax.fori_loop(1, cells_y - 1, inside, 0)

    for piece in range(PIECES):
        at_sides(1, 0, "start", piece)
    at_sides(1, 1, "start")
    gram[...] = jnp.zeros_like(gram)
    for copy in late:
        copy.wait()
    blocks = 4 * cells_x

    def two_sections(pair):
        def products(i, carry):
            inner_products(pair, i)
            return carry

        section(2 * pair + 1)
        lax.fori_loop(0, blocks // 2, products, 0)
        section(2 * pair + 2)
        lax.fori_loop(blocks // 2, blocks, products, 0)

    for pair in range(S // 2):
        two_sections(pair)

    def last_products(i, carry):
        inner_products(S // 2, i, second=False)
        return carry

    lax.fori_loop(0, blocks, last_products, 0)
    save = pltpu.make_async_copy(parts, parts_hbm, save_sem)
    save.start()

    pieces = []
    for pair in range(PAIRS):
        block = gram[pair]
        block = block[:, 0:16] + block[:, 16:32]
        for a in range(pair + 1):
            pieces.append(block[PAIR * a : PAIR * a + 16] + block[PAIR * a + 16 : PAIR * (a + 1)])
    pieces.append(jnp.zeros((16, WIDTH - 16 * len(pieces)), jnp.float32))
    own = jnp.concatenate(pieces, axis=1)

    def exchange(slots, me, count, device, send, recv):
        def copy(step, slot, partner):
            return pltpu.make_async_remote_copy(
                src_ref=slots.at[slot],
                dst_ref=slots.at[slot],
                send_sem=send.at[step],
                recv_sem=recv.at[step],
                device_id=device(partner),
                device_id_type=MESH,
            )

        for step in range(1, count):
            copy(step, me, lax.rem(me + step, count)).start()
        for step in range(1, count):
            source = lax.rem(me + count - step, count)
            copy(step, source, source).wait_recv()
        total = slots[0]
        for slot in range(1, count):
            total = total + slots[slot]
        for step in range(1, count):
            copy(step, me, lax.rem(me + step, count)).wait_send()
        return total

    one[gy] = own
    own = exchange(one, gy, count_y, lambda p: (gx, p), send_one, recv_one)
    two[gx] = own
    total = exchange(two, gx, count_x, lambda p: (p, gy), send_two, recv_two)

    strips = []
    for a in range(PAIRS):
        spots = [pair * (pair + 1) // 2 + a for pair in range(a, PAIRS)]
        strip = [total[:, 16 * spot : 16 * (spot + 1)] for spot in spots]
        if a:
            strip = [jnp.zeros((16, 16 * a), jnp.float32)] + strip
        strip.append(jnp.zeros((16, 128 - 16 * PAIRS), jnp.float32))
        strips.append(jnp.concatenate(strip, axis=1))
    rows = lax.broadcasted_iota(jnp.int32, (COLS, 128), 0)
    columns = lax.broadcasted_iota(jnp.int32, (COLS, 128), 1)
    square = jnp.concatenate(strips + [jnp.zeros((128 - 16 * PAIRS, 128), jnp.float32)], axis=0)
    matrix = square[0:COLS]
    mirror = jnp.transpose(square)[0:COLS]
    matrix = jnp.where(rows // 16 <= columns // 16, matrix, mirror)

    rank = lax.rem(rows, RHS) * STEPS + rows // RHS
    column_rank = lax.rem(columns, RHS) * STEPS + columns // RHS
    inverse = jnp.where(rows == columns, 1.0, 0.0)
    for source in range(RHS):
        places = [k * RHS + source for k in range(STEPS)]
        spread = [jnp.broadcast_to(matrix[:, p : p + 1], (COLS, 128)) for p in places]
        for k, p in enumerate(places):
            order = source * STEPS + k
            row = matrix[p : p + 1, :]
            inverse_row = inverse[p : p + 1, :]
            pivot = spread[k][p : p + 1, :]
            guess = pl.reciprocal(pivot, approx=True)
            guess = guess * (2.0 - pivot * guess)
            over = guess * (2.0 - pivot * guess)
            scale = lax.rsqrt(pivot)
            scale = scale * (1.5 - 0.5 * pivot * scale * scale)
            factor_ref[p : p + 1, :] = jnp.where(
                column_rank[0:1, :] >= order, row * scale, 0.0
            )
            inverse_ref[p : p + 1, :] = inverse_row * scale
            if order + 1 < COLS:
                multiple = jnp.where(rank > order, spread[k], 0.0)
                matrix = matrix - multiple * (row * over)
                inverse = inverse - multiple * (inverse_row * over)
                for l in range(k + 1, STEPS):
                    entry = spread[l][p : p + 1, :] * over
                    spread[l] = spread[l] - multiple * entry
    inverse_ref[COLS:, :] = jnp.zeros((16 * PAIRS - COLS, 128), jnp.float32)

    def finish(k, carry):
        for piece in range(PIECES):
            at_sides(k, 0, "send", piece)
        at_sides(k, 1, "send")
        return carry

    lax.fori_loop(1, STEPS, finish, 0)
    save.wait()


def basis(mask, forcing, flow, shear, counts):
    _, cells_x, cells_y, _ = flow.shape
    cells = (cells_x, cells_y)
    grid_cells = cells_x * cells_y
    count_x, count_y = counts
    dma = pltpu.SemaphoreType.DMA
    height = 16 * PAIRS
    return pl.pallas_call(
        functools.partial(basis_kernel, counts, cells),
        out_shape=(
            jax.ShapeDtypeStruct((4 * cells_x, PAIR * PAIRS, cells_y * 128), jnp.bfloat16),
            jax.ShapeDtypeStruct((height, 128), jnp.float32),
            jax.ShapeDtypeStruct((COLS, 128), jnp.float32),
        ),
        in_specs=[pl.BlockSpec(memory_space=pltpu.HBM)] * 4,
        out_specs=(
            pl.BlockSpec(memory_space=pltpu.HBM),
            pl.BlockSpec(memory_space=VMEM),
            pl.BlockSpec(memory_space=VMEM),
        ),
        scratch_shapes=[
            VMEM((RHS * grid_cells, 128), jnp.int32),
            VMEM((RHS * 4 * grid_cells, 128), jnp.float32),
            VMEM(flow.shape, jnp.float32),
            VMEM(shear.shape, jnp.float32),
            VMEM((4 * cells_x, PAIR * PAIRS, cells_y * 128), jnp.bfloat16),
            VMEM((STEPS + 1, 4, cells_x + 2, cells_y + 2, RHS, 128), jnp.float32),
            VMEM((PAIRS, PAIR * PAIRS, PAIR), jnp.float32),
            VMEM((count_y, 16, WIDTH), jnp.float32),
            VMEM((count_x, 16, WIDTH), jnp.float32),
            dma((STEPS, 2, PIECES)),
            dma((STEPS, 2, PIECES)),
            dma((STEPS, 2)),
            dma((STEPS, 2)),
            dma((count_y,)),
            dma((count_y,)),
            dma((count_x,)),
            dma((count_x,)),
            dma((4,)),
            dma,
        ],
        compiler_params=pltpu.CompilerParams(
            collective_id=0, has_side_effects=True, vmem_limit_bytes=55 * 1024 * 1024
        ),
        name="basis",
    )(
        mask.reshape(RHS * grid_cells, 128),
        forcing.reshape(RHS * 4 * grid_cells, 128),
        flow,
        shear,
    )


def orthonormal_kernel(
    all_cells, cells_y, steps,
    parts_ref, inverse_ref, factor_ref,
    q_ref, r_ref, rms_ref,
    left,
):
    step = pl.program_id(0)
    height = 16 * PAIRS

    @pl.when(step == 0)
    def _():
        column = lax.broadcasted_iota(jnp.int32, (height, PAIR * PAIRS), 1)
        row = lax.broadcasted_iota(jnp.int32, (height, PAIR * PAIRS), 0)
        spread = jnp.where(
            row == 16 * (column // PAIR) + lax.rem(column, 16), 1.0, 0.0
        ).astype(jnp.bfloat16)
        high, middle = split2(inverse_ref[:, 0:height])
        order = permutation(height, height).astype(jnp.bfloat16)
        both = jnp.concatenate(
            [
                jnp.dot(order, part, preferred_element_type=jnp.float32).astype(jnp.bfloat16)
                for part in (high, middle)
            ],
            axis=0,
        )
        left[...] = jnp.dot(both, spread, preferred_element_type=jnp.float32).astype(jnp.bfloat16)

    result = jnp.dot(left[...], parts_ref[0], preferred_element_type=jnp.float32)
    result = result[0:COLS] + result[height : height + COLS]
    q_rows = q_ref.reshape(COLS * cells_y, 128)
    for y in range(cells_y):
        for c in range(0, COLS, 8):
            q_rows[pl.ds(c * cells_y + y, 8, stride=cells_y), :] = result[
                c : c + 8, y * 128 : (y + 1) * 128
            ]

    @pl.when(step == steps - 1)
    def _():
        rows = jnp.dot(
            permutation(COLS, COLS), factor_ref[:, 0:COLS],
            precision=HIGHEST, preferred_element_type=jnp.float32,
        )
        factor = jnp.dot(
            rows, mixing(), precision=HIGHEST, preferred_element_type=jnp.float32
        )
        r_ref[...] = factor
        rms_ref[...] = jnp.sqrt(jnp.sum(factor * factor, axis=0, keepdims=True) / all_cells)


def orthonormal(all_cells, cells, parts, inverse, factor):
    cells_x, cells_y = cells
    steps, depth, width = parts.shape
    height = 16 * PAIRS
    whole = lambda *shape: pl.BlockSpec(shape, lambda i: (0,) * len(shape))
    return pl.pallas_call(
        functools.partial(orthonormal_kernel, all_cells, cells_y, steps),
        grid=(steps,),
        out_shape=(
            jax.ShapeDtypeStruct((COLS, steps, cells_y, 128), jnp.float32),
            jax.ShapeDtypeStruct((COLS, COLS), jnp.float32),
            jax.ShapeDtypeStruct((1, COLS), jnp.float32),
        ),
        in_specs=[
            pl.BlockSpec((1, depth, width), lambda i: (i, 0, 0)),
            whole(height, 128),
            whole(COLS, 128),
        ],
        out_specs=(
            pl.BlockSpec((COLS, 1, cells_y, 128), lambda i: (0, i, 0, 0)),
            whole(COLS, COLS),
            whole(1, COLS),
        ),
        scratch_shapes=[
            VMEM((2 * height, depth), jnp.bfloat16),
        ],
        compiler_params=pltpu.CompilerParams(vmem_limit_bytes=55 * 1024 * 1024),
        name="orthonormal",
    )(parts, inverse, factor)


def shards(actuator_mask, forcing, base_flow, base_shear):
    _, cells_x, cells_y, cells_z = base_flow.shape
    counts = (lax.axis_size("gx"), lax.axis_size("gy"))
    all_cells = 4.0 * cells_x * counts[0] * cells_y * counts[1] * cells_z
    rows, inverse, factor = basis(actuator_mask, forcing, base_flow, base_shear, counts)
    q_basis, r_factor, rms = orthonormal(all_cells, (cells_x, cells_y), rows, inverse, factor)
    return (q_basis.reshape(COLS, 4, cells_x, cells_y, cells_z), r_factor, rms[0])


def solution(mesh):
    return jax.shard_map(
        shards,
        mesh=mesh,
        in_specs=(
            P(None, "gx", "gy", None),
            P(None, None, "gx", "gy", None),
            P(None, "gx", "gy", None),
            P(None, None, "gx", "gy", None),
        ),
        out_specs=(P(None, None, "gx", "gy", None), P(), P()),
        check_vma=False,
    )
```

```python
import functools

import jax
import jax.numpy as jnp
import numpy as np
from jax import lax
from jax.experimental import pallas as pl
from jax.experimental.pallas import tpu as pltpu
from jax.sharding import PartitionSpec as P

S = 8
RHS = 8
STEPS = S + 1
COLS = RHS * STEPS
PAIRS = (STEPS + 1) // 2
PAIR = 32
PIECES = 4
WIDTH = 128 * (-(-8 * PAIRS * (PAIRS + 1) // 128))
VMEM = pltpu.VMEM
MESH = pl.DeviceIdType.MESH
HIGHEST = lax.Precision.HIGHEST

viscosity = 0.04
diffusivity = 0.04
coupling = 0.5
spectral_shift = 0.5

SHIFT = -(6.0 * viscosity + spectral_shift)
BACK = 0.2


def change_of_basis():
    hessenberg = np.zeros((STEPS, STEPS))
    for k in range(STEPS):
        hessenberg[k, k] = SHIFT
        if k + 1 < STEPS:
            hessenberg[k + 1, k] = 1.0
        if k > 0:
            hessenberg[k - 1, k] = -BACK
    change = np.zeros((STEPS, STEPS))
    column = np.zeros(STEPS)
    column[0] = 1.0
    for k in range(STEPS):
        change[:, k] = column
        column = hessenberg @ column
    return change


def place(order):
    source, k = divmod(order, STEPS)
    return k * RHS + source


def permutation(height, width):
    rows = lax.broadcasted_iota(jnp.int32, (height, width), 0)
    columns = lax.broadcasted_iota(jnp.int32, (height, width), 1)
    places = lax.rem(rows, STEPS) * RHS + rows // STEPS
    return jnp.where((places == columns) & (rows < COLS), 1.0, 0.0)


def mixing():
    change = change_of_basis()
    rows = lax.broadcasted_iota(jnp.int32, (COLS, COLS), 0)
    columns = lax.broadcasted_iota(jnp.int32, (COLS, COLS), 1)
    degree = jnp.where(
        lax.rem(rows, RHS) == columns // STEPS, STEPS * (rows // RHS) + lax.rem(columns, STEPS), -1
    )
    mix = jnp.zeros((COLS, COLS), jnp.float32)
    for a in range(STEPS):
        for b in range(a, STEPS):
            mix = jnp.where(degree == STEPS * a + b, float(change[a, b]), mix)
    return mix


def split2(value):
    high = value.astype(jnp.bfloat16)
    return high, (value - high.astype(jnp.float32)).astype(jnp.bfloat16)


def basis_kernel(
    counts, cells,
    mask_hbm, forcing_hbm, flow_hbm, shear_hbm,
    parts_hbm, inverse_ref, factor_ref,
    mask_ref, forcing_ref, flow_ref, shear_ref, parts, fields, gram, one, two,
    send_x, recv_x, send_y, recv_y, send_one, recv_one, send_two, recv_two, load_sem, save_sem,
):
    count_x, count_y = counts
    cells_x, cells_y = cells
    depth = cells_y // PIECES
    gx = lax.axis_index("gx")
    gy = lax.axis_index("gy")

    arrays = (
        (forcing_hbm, forcing_ref), (mask_hbm, mask_ref),
        (flow_hbm, flow_ref), (shear_hbm, shear_ref),
    )
    loads = [pltpu.make_async_copy(a, b, load_sem.at[n]) for n, (a, b) in enumerate(arrays)]
    for copy in loads:
        copy.start()
    early, late = loads[:2], loads[2:]

    barrier = pltpu.get_barrier_semaphore()
    for step in range(1, count_x):
        pl.semaphore_signal(
            barrier, inc=1, device_id=(lax.rem(gx + step, count_x), gy), device_id_type=MESH
        )
    for step in range(1, count_y):
        pl.semaphore_signal(
            barrier, inc=1, device_id=(gx, lax.rem(gy + step, count_y)), device_id_type=MESH
        )

    zero = jnp.zeros((8, 128), jnp.float32)
    lane = lax.broadcasted_iota(jnp.int32, (8, 128), 1)
    first_lane, last_lane = lane == 0, lane == 127

    def clear(k, carry):
        @pl.when(gx == 0)
        def _():
            fields[k, :, 0] = jnp.zeros(fields.shape[1:2] + fields.shape[3:], jnp.float32)

        @pl.when(gx == count_x - 1)
        def _():
            fields[k, :, cells_x + 1] = jnp.zeros(
                fields.shape[1:2] + fields.shape[3:], jnp.float32
            )

        @pl.when(gy == 0)
        def _():
            fields[k, :, :, 0] = jnp.zeros(fields.shape[1:3] + fields.shape[4:], jnp.float32)

        @pl.when(gy == count_y - 1)
        def _():
            fields[k, :, :, cells_y + 1] = jnp.zeros(
                fields.shape[1:3] + fields.shape[4:], jnp.float32
            )

        return carry

    lax.fori_loop(1, STEPS, clear, 0)
    fields[0] = jnp.zeros(fields.shape[1:], jnp.float32)

    def start_row(i, carry):
        x, y = i // cells_y, lax.rem(i, cells_y)
        mask = mask_ref[pl.ds(i, RHS, stride=cells_x * cells_y), :].astype(jnp.float32)
        for f in range(4):
            where = f * cells_x * cells_y + i
            value = forcing_ref[pl.ds(where, RHS, stride=4 * cells_x * cells_y), :]
            fields[1, f, x + 1, y + 1] = value * mask
        return carry

    for copy in early:
        copy.wait()
    lax.fori_loop(0, cells_x * cells_y, start_row, 0)
    pl.semaphore_wait(barrier, count_x + count_y - 2)

    def halo(k, axis, up, piece):
        side = 1 if up else 0
        if axis == 0:
            source = cells_x if up else 1
            target = 0 if up else cells_x + 1
            rows = pl.ds(1 + piece * depth, depth)
            return pltpu.make_async_remote_copy(
                src_ref=fields.at[k, :, source, rows],
                dst_ref=fields.at[k, :, target, rows],
                send_sem=send_x.at[k, side, piece],
                recv_sem=recv_x.at[k, side, piece],
                device_id=(gx + 1 if up else gx - 1, gy),
                device_id_type=MESH,
            )
        source = cells_y if up else 1
        target = 0 if up else cells_y + 1
        rows = pl.ds(1, cells_x)
        return pltpu.make_async_remote_copy(
            src_ref=fields.at[k, :, rows, source],
            dst_ref=fields.at[k, :, rows, target],
            send_sem=send_y.at[k, side],
            recv_sem=recv_y.at[k, side],
            device_id=(gx, gy + 1 if up else gy - 1),
            device_id_type=MESH,
        )

    def at_sides(k, axis, what, piece=0):
        me, count = (gx, count_x) if axis == 0 else (gy, count_y)
        for up in (True, False):
            sends = me < count - 1 if up else me > 0
            receives = me > 0 if up else me < count - 1

            @pl.when(receives if what == "recv" else sends)
            def _(up=up):
                copy = halo(k, axis, up, piece)
                if what == "start":
                    copy.start()
                elif what == "send":
                    copy.wait_send()
                else:
                    copy.wait_recv()

    def advance(k, x, y):
        def value(f, dx=0, dy=0):
            return fields[k, f, x + 1 + dx, y + 1 + dy]

        centre = [value(f) for f in range(4)]
        plus = [
            [value(f, 1, 0) for f in range(4)],
            [value(f, 0, 1) for f in range(4)],
            [jnp.where(last_lane, zero, pltpu.roll(centre[f], 127, 1)) for f in range(4)],
        ]
        minus = [
            [value(f, -1, 0) for f in range(4)],
            [value(f, 0, -1) for f in range(4)],
            [jnp.where(first_lane, zero, pltpu.roll(centre[f], 1, 1)) for f in range(4)],
        ]
        result = [BACK * fields[k - 1, f, x + 1, y + 1] for f in range(4)]
        for j in range(3):
            half = 0.5 * flow_ref[j, x, pl.ds(y, 1), :]
            ahead = jnp.broadcast_to(viscosity - half, (8, 128))
            behind = jnp.broadcast_to(viscosity + half, (8, 128))
            for i in range(3):
                result[i] = result[i] + ahead * plus[j][i] + behind * minus[j][i]
                shear = jnp.broadcast_to(shear_ref[i, j, x, pl.ds(y, 1), :], (8, 128))
                result[i] = result[i] - shear * centre[j]
            result[j] = result[j] - 0.5 * (plus[j][3] - minus[j][3])
            result[3] = result[3] + diffusivity * (plus[j][3] + minus[j][3])
            result[3] = result[3] - (0.5 * coupling) * (plus[j][j] - minus[j][j])
        for f in range(4):
            fields[k + 1, f, x + 1, y + 1] = result[f]

    def inner_products(pair, i, second=True):
        f, x = i // cells_x, lax.rem(i, cells_x)
        k = 2 * pair + 1
        first = jnp.concatenate([fields[k, f, x + 1, y + 1] for y in range(cells_y)], axis=1)
        if second:
            other = jnp.concatenate(
                [fields[k + 1, f, x + 1, y + 1] for y in range(cells_y)], axis=1
            )
        else:
            other = jnp.zeros_like(first)
        new = jnp.concatenate(split2(jnp.concatenate([first, other], axis=0)), axis=0)
        parts[i, PAIR * pair : PAIR * (pair + 1), :] = new
        below = slice(0, PAIR * (pair + 1))
        gram[pair, below] += lax.dot_general(
            parts[i, below], new, (((1,), (1,)), ((), ())), preferred_element_type=jnp.float32
        )

    def section(k):
        def y_faces(x, carry):
            advance(k, x, 0)
            advance(k, x, cells_y - 1)
            return carry

        def inside(y, carry):
            for x in range(1, cells_x - 1):
                advance(k, x, y)
            return carry

        def piece_of_faces(piece, carry):
            at_sides(k, 0, "recv", piece)
            for y in range(depth):
                advance(k, 0, piece * depth + y)
                advance(k, cells_x - 1, piece * depth + y)

            if k < S:
                at_sides(k + 1, 0, "start", piece)

            return carry

        at_sides(k, 1, "recv")
        lax.fori_loop(0, PIECES, piece_of_faces, 0)
        lax.fori_loop(1, cells_x - 1, y_faces, 0)

        if k < S:
            at_sides(k + 1, 1, "start")

        lax.fori_loop(1, cells_y - 1, inside, 0)

    for piece in range(PIECES):
        at_sides(1, 0, "start", piece)
    at_sides(1, 1, "start")
    gram[...] = jnp.zeros_like(gram)
    for copy in late:
        copy.wait()
    blocks = 4 * cells_x

    def two_sections(pair):
        def products(i, carry):
            inner_products(pair, i)
            return carry

        section(2 * pair + 1)
        lax.fori_loop(0, blocks // 2, products, 0)
        section(2 * pair + 2)
        lax.fori_loop(blocks // 2, blocks, products, 0)

    for pair in range(S // 2):
        two_sections(pair)

    def last_products(i, carry):
        inner_products(S // 2, i, second=False)
        return carry

    lax.fori_loop(0, blocks, last_products, 0)
    save = pltpu.make_async_copy(parts, parts_hbm, save_sem)
    save.start()

    pieces = []
    for pair in range(PAIRS):
        block = gram[pair]
        block = block[:, 0:16] + block[:, 16:32]
        for a in range(pair + 1):
            pieces.append(block[PAIR * a : PAIR * a + 16] + block[PAIR * a + 16 : PAIR * (a + 1)])
    pieces.append(jnp.zeros((16, WIDTH - 16 * len(pieces)), jnp.float32))
    own = jnp.concatenate(pieces, axis=1)

    def exchange(slots, me, count, device, send, recv):
        def copy(step, slot, partner):
            return pltpu.make_async_remote_copy(
                src_ref=slots.at[slot],
                dst_ref=slots.at[slot],
                send_sem=send.at[step],
                recv_sem=recv.at[step],
                device_id=device(partner),
                device_id_type=MESH,
            )

        for step in range(1, count):
            copy(step, me, lax.rem(me + step, count)).start()
        for step in range(1, count):
            source = lax.rem(me + count - step, count)
            copy(step, source, source).wait_recv()
        total = slots[0]
        for slot in range(1, count):
            total = total + slots[slot]
        for step in range(1, count):
            copy(step, me, lax.rem(me + step, count)).wait_send()
        return total

    one[gy] = own
    own = exchange(one, gy, count_y, lambda p: (gx, p), send_one, recv_one)
    two[gx] = own
    total = exchange(two, gx, count_x, lambda p: (p, gy), send_two, recv_two)

    strips = []
    for a in range(PAIRS):
        spots = [pair * (pair + 1) // 2 + a for pair in range(a, PAIRS)]
        strip = [total[:, 16 * spot : 16 * (spot + 1)] for spot in spots]
        if a:
            strip = [jnp.zeros((16, 16 * a), jnp.float32)] + strip
        strip.append(jnp.zeros((16, 128 - 16 * PAIRS), jnp.float32))
        strips.append(jnp.concatenate(strip, axis=1))
    rows = lax.broadcasted_iota(jnp.int32, (COLS, 128), 0)
    columns = lax.broadcasted_iota(jnp.int32, (COLS, 128), 1)
    square = jnp.concatenate(strips + [jnp.zeros((128 - 16 * PAIRS, 128), jnp.float32)], axis=0)
    matrix = square[0:COLS]
    mirror = jnp.transpose(square)[0:COLS]
    matrix = jnp.where(rows // 16 <= columns // 16, matrix, mirror)

    rank = lax.rem(rows, RHS) * STEPS + rows // RHS
    column_rank = lax.rem(columns, RHS) * STEPS + columns // RHS
    inverse = jnp.where(rows == columns, 1.0, 0.0)
    for source in range(RHS):
        places = [k * RHS + source for k in range(STEPS)]
        spread = [jnp.broadcast_to(matrix[:, p : p + 1], (COLS, 128)) for p in places]
        for k, p in enumerate(places):
            order = source * STEPS + k
            row = matrix[p : p + 1, :]
            inverse_row = inverse[p : p + 1, :]
            pivot = spread[k][p : p + 1, :]
            guess = pl.reciprocal(pivot, approx=True)
            guess = guess * (2.0 - pivot * guess)
            over = guess * (2.0 - pivot * guess)
            scale = lax.rsqrt(pivot)
            scale = scale * (1.5 - 0.5 * pivot * scale * scale)
            factor_ref[p : p + 1, :] = jnp.where(
                column_rank[0:1, :] >= order, row * scale, 0.0
            )
            inverse_ref[p : p + 1, :] = inverse_row * scale
            if order + 1 < COLS:
                multiple = jnp.where(rank > order, spread[k], 0.0)
                matrix = matrix - multiple * (row * over)
                inverse = inverse - multiple * (inverse_row * over)
                for l in range(k + 1, STEPS):
                    entry = spread[l][p : p + 1, :] * over
                    spread[l] = spread[l] - multiple * entry
    inverse_ref[COLS:, :] = jnp.zeros((16 * PAIRS - COLS, 128), jnp.float32)

    def finish(k, carry):
        for piece in range(PIECES):
            at_sides(k, 0, "send", piece)
        at_sides(k, 1, "send")
        return carry

    lax.fori_loop(1, STEPS, finish, 0)
    save.wait()


def basis(mask, forcing, flow, shear, counts):
    _, cells_x, cells_y, _ = flow.shape
    cells = (cells_x, cells_y)
    grid_cells = cells_x * cells_y
    count_x, count_y = counts
    dma = pltpu.SemaphoreType.DMA
    height = 16 * PAIRS
    return pl.pallas_call(
        functools.partial(basis_kernel, counts, cells),
        out_shape=(
            jax.ShapeDtypeStruct((4 * cells_x, PAIR * PAIRS, cells_y * 128), jnp.bfloat16),
            jax.ShapeDtypeStruct((height, 128), jnp.float32),
            jax.ShapeDtypeStruct((COLS, 128), jnp.float32),
        ),
        in_specs=[pl.BlockSpec(memory_space=pltpu.HBM)] * 4,
        out_specs=(
            pl.BlockSpec(memory_space=pltpu.HBM),
            pl.BlockSpec(memory_space=VMEM),
            pl.BlockSpec(memory_space=VMEM),
        ),
        scratch_shapes=[
            VMEM((RHS * grid_cells, 128), jnp.int32),
            VMEM((RHS * 4 * grid_cells, 128), jnp.float32),
            VMEM(flow.shape, jnp.float32),
            VMEM(shear.shape, jnp.float32),
            VMEM((4 * cells_x, PAIR * PAIRS, cells_y * 128), jnp.bfloat16),
            VMEM((STEPS + 1, 4, cells_x + 2, cells_y + 2, RHS, 128), jnp.float32),
            VMEM((PAIRS, PAIR * PAIRS, PAIR), jnp.float32),
            VMEM((count_y, 16, WIDTH), jnp.float32),
            VMEM((count_x, 16, WIDTH), jnp.float32),
            dma((STEPS, 2, PIECES)),
            dma((STEPS, 2, PIECES)),
            dma((STEPS, 2)),
            dma((STEPS, 2)),
            dma((count_y,)),
            dma((count_y,)),
            dma((count_x,)),
            dma((count_x,)),
            dma((4,)),
            dma,
        ],
        compiler_params=pltpu.CompilerParams(
            collective_id=0, has_side_effects=True, vmem_limit_bytes=55 * 1024 * 1024
        ),
        name="basis",
    )(
        mask.reshape(RHS * grid_cells, 128),
        forcing.reshape(RHS * 4 * grid_cells, 128),
        flow,
        shear,
    )


def orthonormal_kernel(
    all_cells, cells_y, blocks, group,
    parts_hbm, inverse_ref, factor_ref,
    q_hbm, r_ref, rms_ref,
    left, parts, q, load_sem, save_sem,
):
    height = 16 * PAIRS

    def load(n):
        span = pl.ds(n * group, group)
        return pltpu.make_async_copy(parts_hbm.at[span], parts.at[span], load_sem.at[n])

    def save(n):
        span = pl.ds(n * group, group)
        return pltpu.make_async_copy(q.at[:, span], q_hbm.at[:, span], save_sem.at[n])

    for n in range(blocks // group):
        load(n).start()

    column = lax.broadcasted_iota(jnp.int32, (height, PAIR * PAIRS), 1)
    row = lax.broadcasted_iota(jnp.int32, (height, PAIR * PAIRS), 0)
    spread = jnp.where(
        row == 16 * (column // PAIR) + lax.rem(column, 16), 1.0, 0.0
    ).astype(jnp.bfloat16)
    high, middle = split2(inverse_ref[:, 0:height])
    order = permutation(height, height).astype(jnp.bfloat16)
    both = jnp.concatenate(
        [
            jnp.dot(order, part, preferred_element_type=jnp.float32).astype(jnp.bfloat16)
            for part in (high, middle)
        ],
        axis=0,
    )
    left[...] = jnp.dot(both, spread, preferred_element_type=jnp.float32).astype(jnp.bfloat16)
    q_rows = q.reshape(COLS * blocks * cells_y, 128)

    def some(n, carry):
        load(n).wait()
        for inner in range(group):
            i = n * group + inner
            result = jnp.dot(left[...], parts[i], preferred_element_type=jnp.float32)
            result = result[0:COLS] + result[height : height + COLS]
            for y in range(cells_y):
                for c in range(0, COLS, 8):
                    where = (c * blocks + i) * cells_y + y
                    q_rows[pl.ds(where, 8, stride=blocks * cells_y), :] = result[
                        c : c + 8, y * 128 : (y + 1) * 128
                    ]
        save(n).start()
        return carry

    lax.fori_loop(0, blocks // group, some, 0)
    rows = jnp.dot(
        permutation(COLS, COLS), factor_ref[:, 0:COLS],
        precision=HIGHEST, preferred_element_type=jnp.float32,
    )
    factor = jnp.dot(rows, mixing(), precision=HIGHEST, preferred_element_type=jnp.float32)
    r_ref[...] = factor
    rms_ref[...] = jnp.sqrt(jnp.sum(factor * factor, axis=0, keepdims=True) / all_cells)
    for n in range(blocks // group):
        save(n).wait()


def orthonormal(all_cells, cells, parts, inverse, factor):
    cells_x, cells_y = cells
    blocks, depth, width = parts.shape
    group = 2
    height = 16 * PAIRS
    return pl.pallas_call(
        functools.partial(orthonormal_kernel, all_cells, cells_y, blocks, group),
        out_shape=(
            jax.ShapeDtypeStruct((COLS, blocks, cells_y, 128), jnp.float32),
            jax.ShapeDtypeStruct((COLS, COLS), jnp.float32),
            jax.ShapeDtypeStruct((1, COLS), jnp.float32),
        ),
        in_specs=[
            pl.BlockSpec(memory_space=pltpu.HBM),
            pl.BlockSpec(memory_space=VMEM),
            pl.BlockSpec(memory_space=VMEM),
        ],
        out_specs=(
            pl.BlockSpec(memory_space=pltpu.HBM),
            pl.BlockSpec(memory_space=VMEM),
            pl.BlockSpec(memory_space=VMEM),
        ),
        scratch_shapes=[
            VMEM((2 * height, depth), jnp.bfloat16),
            VMEM(parts.shape, jnp.bfloat16),
            VMEM((COLS, blocks, cells_y, 128), jnp.float32),
            pltpu.SemaphoreType.DMA((blocks // group,)),
            pltpu.SemaphoreType.DMA((blocks // group,)),
        ],
        compiler_params=pltpu.CompilerParams(vmem_limit_bytes=55 * 1024 * 1024),
        name="orthonormal",
    )(parts, inverse, factor)


def shards(actuator_mask, forcing, base_flow, base_shear):
    _, cells_x, cells_y, cells_z = base_flow.shape
    counts = (lax.axis_size("gx"), lax.axis_size("gy"))
    all_cells = 4.0 * cells_x * counts[0] * cells_y * counts[1] * cells_z
    rows, inverse, factor = basis(actuator_mask, forcing, base_flow, base_shear, counts)
    q_basis, r_factor, rms = orthonormal(all_cells, (cells_x, cells_y), rows, inverse, factor)
    return (q_basis.reshape(COLS, 4, cells_x, cells_y, cells_z), r_factor, rms[0])


def solution(mesh):
    return jax.shard_map(
        shards,
        mesh=mesh,
        in_specs=(
            P(None, "gx", "gy", None),
            P(None, None, "gx", "gy", None),
            P(None, "gx", "gy", None),
            P(None, None, "gx", "gy", None),
        ),
        out_specs=(P(None, None, "gx", "gy", None), P(), P()),
        check_vma=False,
    )
```

```python
import functools

import jax
import jax.numpy as jnp
import numpy as np
from jax import lax
from jax.experimental import pallas as pl
from jax.experimental.pallas import tpu as pltpu
from jax.sharding import PartitionSpec as P

S = 8
RHS = 8
STEPS = S + 1
COLS = RHS * STEPS
PAIRS = (STEPS + 1) // 2
PAIR = 32
PIECES = 4
WIDTH = 128 * (-(-8 * PAIRS * (PAIRS + 1) // 128))
VMEM = pltpu.VMEM
MESH = pl.DeviceIdType.MESH
HIGHEST = lax.Precision.HIGHEST

viscosity = 0.04
diffusivity = 0.04
coupling = 0.5
spectral_shift = 0.5

SHIFT = -(6.0 * viscosity + spectral_shift)
BACK = 0.2


def change_of_basis():
    hessenberg = np.zeros((STEPS, STEPS))
    for k in range(STEPS):
        hessenberg[k, k] = SHIFT
        if k + 1 < STEPS:
            hessenberg[k + 1, k] = 1.0
        if k > 0:
            hessenberg[k - 1, k] = -BACK
    change = np.zeros((STEPS, STEPS))
    column = np.zeros(STEPS)
    column[0] = 1.0
    for k in range(STEPS):
        change[:, k] = column
        column = hessenberg @ column
    return change


def place(order):
    source, k = divmod(order, STEPS)
    return k * RHS + source


def permutation(height, width):
    rows = lax.broadcasted_iota(jnp.int32, (height, width), 0)
    columns = lax.broadcasted_iota(jnp.int32, (height, width), 1)
    places = lax.rem(rows, STEPS) * RHS + rows // STEPS
    return jnp.where((places == columns) & (rows < COLS), 1.0, 0.0)


def mixing():
    change = change_of_basis()
    rows = lax.broadcasted_iota(jnp.int32, (COLS, COLS), 0)
    columns = lax.broadcasted_iota(jnp.int32, (COLS, COLS), 1)
    degree = jnp.where(
        lax.rem(rows, RHS) == columns // STEPS, STEPS * (rows // RHS) + lax.rem(columns, STEPS), -1
    )
    mix = jnp.zeros((COLS, COLS), jnp.float32)
    for a in range(STEPS):
        for b in range(a, STEPS):
            mix = jnp.where(degree == STEPS * a + b, float(change[a, b]), mix)
    return mix


def split2(value):
    high = value.astype(jnp.bfloat16)
    return high, (value - high.astype(jnp.float32)).astype(jnp.bfloat16)


def basis_kernel(
    counts, cells,
    mask_hbm, forcing_hbm, flow_hbm, shear_hbm,
    parts_hbm, inverse_ref, factor_ref,
    mask_ref, forcing_ref, flow_ref, shear_ref, parts, fields, gram, one, two,
    send_x, recv_x, send_y, recv_y, send_one, recv_one, send_two, recv_two, load_sem, save_sem,
):
    count_x, count_y = counts
    cells_x, cells_y = cells
    depth = cells_y // PIECES
    gx = lax.axis_index("gx")
    gy = lax.axis_index("gy")

    arrays = (
        (forcing_hbm, forcing_ref), (mask_hbm, mask_ref),
        (flow_hbm, flow_ref), (shear_hbm, shear_ref),
    )
    loads = [pltpu.make_async_copy(a, b, load_sem.at[n]) for n, (a, b) in enumerate(arrays)]
    for copy in loads:
        copy.start()
    early, late = loads[:2], loads[2:]

    barrier = pltpu.get_barrier_semaphore()
    for step in range(1, count_x):
        pl.semaphore_signal(
            barrier, inc=1, device_id=(lax.rem(gx + step, count_x), gy), device_id_type=MESH
        )
    for step in range(1, count_y):
        pl.semaphore_signal(
            barrier, inc=1, device_id=(gx, lax.rem(gy + step, count_y)), device_id_type=MESH
        )

    zero = jnp.zeros((8, 128), jnp.float32)
    lane = lax.broadcasted_iota(jnp.int32, (8, 128), 1)
    first_lane, last_lane = lane == 0, lane == 127

    def clear(k, carry):
        @pl.when(gx == 0)
        def _():
            fields[k, :, 0] = jnp.zeros(fields.shape[1:2] + fields.shape[3:], jnp.float32)

        @pl.when(gx == count_x - 1)
        def _():
            fields[k, :, cells_x + 1] = jnp.zeros(
                fields.shape[1:2] + fields.shape[3:], jnp.float32
            )

        @pl.when(gy == 0)
        def _():
            fields[k, :, :, 0] = jnp.zeros(fields.shape[1:3] + fields.shape[4:], jnp.float32)

        @pl.when(gy == count_y - 1)
        def _():
            fields[k, :, :, cells_y + 1] = jnp.zeros(
                fields.shape[1:3] + fields.shape[4:], jnp.float32
            )

        return carry

    lax.fori_loop(1, STEPS, clear, 0)
    fields[0] = jnp.zeros(fields.shape[1:], jnp.float32)

    def start_row(i, carry):
        x, y = i // cells_y, lax.rem(i, cells_y)
        mask = mask_ref[pl.ds(i, RHS, stride=cells_x * cells_y), :].astype(jnp.float32)
        for f in range(4):
            where = f * cells_x * cells_y + i
            value = forcing_ref[pl.ds(where, RHS, stride=4 * cells_x * cells_y), :]
            fields[1, f, x + 1, y + 1] = value * mask
        return carry

    for copy in early:
        copy.wait()
    lax.fori_loop(0, cells_x * cells_y, start_row, 0)
    pl.semaphore_wait(barrier, count_x + count_y - 2)

    def halo(k, axis, up, piece):
        side = 1 if up else 0
        if axis == 0:
            source = cells_x if up else 1
            target = 0 if up else cells_x + 1
            rows = pl.ds(1 + piece * depth, depth)
            return pltpu.make_async_remote_copy(
                src_ref=fields.at[k, :, source, rows],
                dst_ref=fields.at[k, :, target, rows],
                send_sem=send_x.at[k, side, piece],
                recv_sem=recv_x.at[k, side, piece],
                device_id=(gx + 1 if up else gx - 1, gy),
                device_id_type=MESH,
            )
        source = cells_y if up else 1
        target = 0 if up else cells_y + 1
        rows = pl.ds(1, cells_x)
        return pltpu.make_async_remote_copy(
            src_ref=fields.at[k, :, rows, source],
            dst_ref=fields.at[k, :, rows, target],
            send_sem=send_y.at[k, side],
            recv_sem=recv_y.at[k, side],
            device_id=(gx, gy + 1 if up else gy - 1),
            device_id_type=MESH,
        )

    def at_sides(k, axis, what, piece=0):
        me, count = (gx, count_x) if axis == 0 else (gy, count_y)
        for up in (True, False):
            sends = me < count - 1 if up else me > 0
            receives = me > 0 if up else me < count - 1

            @pl.when(receives if what == "recv" else sends)
            def _(up=up):
                copy = halo(k, axis, up, piece)
                if what == "start":
                    copy.start()
                elif what == "send":
                    copy.wait_send()
                else:
                    copy.wait_recv()

    def advance(k, x, y):
        def value(f, dx=0, dy=0):
            return fields[k, f, x + 1 + dx, y + 1 + dy]

        centre = [value(f) for f in range(4)]
        plus = [
            [value(f, 1, 0) for f in range(4)],
            [value(f, 0, 1) for f in range(4)],
            [jnp.where(last_lane, zero, pltpu.roll(centre[f], 127, 1)) for f in range(4)],
        ]
        minus = [
            [value(f, -1, 0) for f in range(4)],
            [value(f, 0, -1) for f in range(4)],
            [jnp.where(first_lane, zero, pltpu.roll(centre[f], 1, 1)) for f in range(4)],
        ]
        result = [BACK * fields[k - 1, f, x + 1, y + 1] for f in range(4)]
        for j in range(3):
            half = 0.5 * flow_ref[j, x, pl.ds(y, 1), :]
            ahead = jnp.broadcast_to(viscosity - half, (8, 128))
            behind = jnp.broadcast_to(viscosity + half, (8, 128))
            for i in range(3):
                result[i] = result[i] + ahead * plus[j][i] + behind * minus[j][i]
                shear = jnp.broadcast_to(shear_ref[i, j, x, pl.ds(y, 1), :], (8, 128))
                result[i] = result[i] - shear * centre[j]
            result[j] = result[j] - 0.5 * (plus[j][3] - minus[j][3])
            result[3] = result[3] + diffusivity * (plus[j][3] + minus[j][3])
            result[3] = result[3] - (0.5 * coupling) * (plus[j][j] - minus[j][j])
        for f in range(4):
            fields[k + 1, f, x + 1, y + 1] = result[f]

    def inner_products(pair, i, second=True):
        f, x = i // cells_x, lax.rem(i, cells_x)
        k = 2 * pair + 1
        first = jnp.concatenate([fields[k, f, x + 1, y + 1] for y in range(cells_y)], axis=1)
        if second:
            other = jnp.concatenate(
                [fields[k + 1, f, x + 1, y + 1] for y in range(cells_y)], axis=1
            )
        else:
            other = jnp.zeros_like(first)
        new = jnp.concatenate(split2(jnp.concatenate([first, other], axis=0)), axis=0)
        parts[i, PAIR * pair : PAIR * (pair + 1), :] = new
        below = slice(0, PAIR * (pair + 1))
        gram[pair, below] += lax.dot_general(
            parts[i, below], new, (((1,), (1,)), ((), ())), preferred_element_type=jnp.float32
        )

    def section(k):
        def y_faces(x, carry):
            advance(k, x, 0)
            advance(k, x, cells_y - 1)
            return carry

        def inside(y, carry):
            for x in range(1, cells_x - 1):
                advance(k, x, y)
            return carry

        def piece_of_faces(piece, carry):
            at_sides(k, 0, "recv", piece)
            for y in range(depth):
                advance(k, 0, piece * depth + y)
                advance(k, cells_x - 1, piece * depth + y)

            if k < S:
                at_sides(k + 1, 0, "start", piece)

            return carry

        lax.fori_loop(1, PIECES - 1, piece_of_faces, 0)
        at_sides(k, 1, "recv")
        piece_of_faces(0, 0)
        piece_of_faces(PIECES - 1, 0)
        lax.fori_loop(1, cells_x - 1, y_faces, 0)

        if k < S:
            at_sides(k + 1, 1, "start")

        lax.fori_loop(1, cells_y - 1, inside, 0)

    for piece in (*range(1, PIECES - 1), 0, PIECES - 1):
        at_sides(1, 0, "start", piece)
    at_sides(1, 1, "start")
    gram[...] = jnp.zeros_like(gram)
    for copy in late:
        copy.wait()
    blocks = 4 * cells_x

    def two_sections(pair):
        def products(i, carry):
            inner_products(pair, i)
            return carry

        section(2 * pair + 1)
        lax.fori_loop(0, blocks // 2, products, 0)
        section(2 * pair + 2)
        lax.fori_loop(blocks // 2, blocks, products, 0)

    for pair in range(S // 2):
        two_sections(pair)

    def last_products(i, carry):
        inner_products(S // 2, i, second=False)
        return carry

    lax.fori_loop(0, blocks, last_products, 0)
    save = pltpu.make_async_copy(parts, parts_hbm, save_sem)
    save.start()

    pieces = []
    for pair in range(PAIRS):
        block = gram[pair]
        block = block[:, 0:16] + block[:, 16:32]
        for a in range(pair + 1):
            pieces.append(block[PAIR * a : PAIR * a + 16] + block[PAIR * a + 16 : PAIR * (a + 1)])
    pieces.append(jnp.zeros((16, WIDTH - 16 * len(pieces)), jnp.float32))
    own = jnp.concatenate(pieces, axis=1)

    def exchange(slots, me, count, device, send, recv):
        def copy(step, slot, partner):
            return pltpu.make_async_remote_copy(
                src_ref=slots.at[slot],
                dst_ref=slots.at[slot],
                send_sem=send.at[step],
                recv_sem=recv.at[step],
                device_id=device(partner),
                device_id_type=MESH,
            )

        for step in range(1, count):
            copy(step, me, lax.rem(me + step, count)).start()
        for step in range(1, count):
            source = lax.rem(me + count - step, count)
            copy(step, source, source).wait_recv()
        total = slots[0]
        for slot in range(1, count):
            total = total + slots[slot]
        for step in range(1, count):
            copy(step, me, lax.rem(me + step, count)).wait_send()
        return total

    one[gy] = own
    own = exchange(one, gy, count_y, lambda p: (gx, p), send_one, recv_one)
    two[gx] = own
    total = exchange(two, gx, count_x, lambda p: (p, gy), send_two, recv_two)

    strips = []
    for a in range(PAIRS):
        spots = [pair * (pair + 1) // 2 + a for pair in range(a, PAIRS)]
        strip = [total[:, 16 * spot : 16 * (spot + 1)] for spot in spots]
        if a:
            strip = [jnp.zeros((16, 16 * a), jnp.float32)] + strip
        strip.append(jnp.zeros((16, 128 - 16 * PAIRS), jnp.float32))
        strips.append(jnp.concatenate(strip, axis=1))
    rows = lax.broadcasted_iota(jnp.int32, (COLS, 128), 0)
    columns = lax.broadcasted_iota(jnp.int32, (COLS, 128), 1)
    square = jnp.concatenate(strips + [jnp.zeros((128 - 16 * PAIRS, 128), jnp.float32)], axis=0)
    matrix = square[0:COLS]
    mirror = jnp.transpose(square)[0:COLS]
    matrix = jnp.where(rows // 16 <= columns // 16, matrix, mirror)

    rank = lax.rem(rows, RHS) * STEPS + rows // RHS
    column_rank = lax.rem(columns, RHS) * STEPS + columns // RHS
    inverse = jnp.where(rows == columns, 1.0, 0.0)
    for source in range(RHS):
        places = [k * RHS + source for k in range(STEPS)]
        spread = [jnp.broadcast_to(matrix[:, p : p + 1], (COLS, 128)) for p in places]
        for k, p in enumerate(places):
            order = source * STEPS + k
            row = matrix[p : p + 1, :]
            inverse_row = inverse[p : p + 1, :]
            pivot = spread[k][p : p + 1, :]
            guess = pl.reciprocal(pivot, approx=True)
            guess = guess * (2.0 - pivot * guess)
            over = guess * (2.0 - pivot * guess)
            scale = lax.rsqrt(pivot)
            scale = scale * (1.5 - 0.5 * pivot * scale * scale)
            factor_ref[p : p + 1, :] = jnp.where(
                column_rank[0:1, :] >= order, row * scale, 0.0
            )
            inverse_ref[p : p + 1, :] = inverse_row * scale
            if order + 1 < COLS:
                multiple = jnp.where(rank > order, spread[k], 0.0)
                matrix = matrix - multiple * (row * over)
                inverse = inverse - multiple * (inverse_row * over)
                for l in range(k + 1, STEPS):
                    entry = spread[l][p : p + 1, :] * over
                    spread[l] = spread[l] - multiple * entry
    inverse_ref[COLS:, :] = jnp.zeros((16 * PAIRS - COLS, 128), jnp.float32)

    def finish(k, carry):
        for piece in range(PIECES):
            at_sides(k, 0, "send", piece)
        at_sides(k, 1, "send")
        return carry

    lax.fori_loop(1, STEPS, finish, 0)
    save.wait()


def basis(mask, forcing, flow, shear, counts):
    _, cells_x, cells_y, _ = flow.shape
    cells = (cells_x, cells_y)
    grid_cells = cells_x * cells_y
    count_x, count_y = counts
    dma = pltpu.SemaphoreType.DMA
    height = 16 * PAIRS
    return pl.pallas_call(
        functools.partial(basis_kernel, counts, cells),
        out_shape=(
            jax.ShapeDtypeStruct((4 * cells_x, PAIR * PAIRS, cells_y * 128), jnp.bfloat16),
            jax.ShapeDtypeStruct((height, 128), jnp.float32),
            jax.ShapeDtypeStruct((COLS, 128), jnp.float32),
        ),
        in_specs=[pl.BlockSpec(memory_space=pltpu.HBM)] * 4,
        out_specs=(
            pl.BlockSpec(memory_space=pltpu.HBM),
            pl.BlockSpec(memory_space=VMEM),
            pl.BlockSpec(memory_space=VMEM),
        ),
        scratch_shapes=[
            VMEM((RHS * grid_cells, 128), jnp.int32),
            VMEM((RHS * 4 * grid_cells, 128), jnp.float32),
            VMEM(flow.shape, jnp.float32),
            VMEM(shear.shape, jnp.float32),
            VMEM((4 * cells_x, PAIR * PAIRS, cells_y * 128), jnp.bfloat16),
            VMEM((STEPS + 1, 4, cells_x + 2, cells_y + 2, RHS, 128), jnp.float32),
            VMEM((PAIRS, PAIR * PAIRS, PAIR), jnp.float32),
            VMEM((count_y, 16, WIDTH), jnp.float32),
            VMEM((count_x, 16, WIDTH), jnp.float32),
            dma((STEPS, 2, PIECES)),
            dma((STEPS, 2, PIECES)),
            dma((STEPS, 2)),
            dma((STEPS, 2)),
            dma((count_y,)),
            dma((count_y,)),
            dma((count_x,)),
            dma((count_x,)),
            dma((4,)),
            dma,
        ],
        compiler_params=pltpu.CompilerParams(
            collective_id=0, has_side_effects=True, vmem_limit_bytes=55 * 1024 * 1024
        ),
        name="basis",
    )(
        mask.reshape(RHS * grid_cells, 128),
        forcing.reshape(RHS * 4 * grid_cells, 128),
        flow,
        shear,
    )


def orthonormal_kernel(
    all_cells, cells_y, blocks, group,
    parts_hbm, inverse_ref, factor_ref,
    q_hbm, r_ref, rms_ref,
    left, parts, q, load_sem, save_sem,
):
    height = 16 * PAIRS

    def load(n):
        span = pl.ds(n * group, group)
        return pltpu.make_async_copy(parts_hbm.at[span], parts.at[span], load_sem.at[n])

    def save(n):
        span = pl.ds(n * group, group)
        return pltpu.make_async_copy(q.at[:, span], q_hbm.at[:, span], save_sem.at[n])

    for n in range(blocks // group):
        load(n).start()

    column = lax.broadcasted_iota(jnp.int32, (height, PAIR * PAIRS), 1)
    row = lax.broadcasted_iota(jnp.int32, (height, PAIR * PAIRS), 0)
    spread = jnp.where(
        row == 16 * (column // PAIR) + lax.rem(column, 16), 1.0, 0.0
    ).astype(jnp.bfloat16)
    high, middle = split2(inverse_ref[:, 0:height])
    order = permutation(height, height).astype(jnp.bfloat16)
    both = jnp.concatenate(
        [
            jnp.dot(order, part, preferred_element_type=jnp.float32).astype(jnp.bfloat16)
            for part in (high, middle)
        ],
        axis=0,
    )
    left[...] = jnp.dot(both, spread, preferred_element_type=jnp.float32).astype(jnp.bfloat16)
    q_rows = q.reshape(COLS * blocks * cells_y, 128)

    def some(n, carry):
        load(n).wait()
        for inner in range(group):
            i = n * group + inner
            result = jnp.dot(left[...], parts[i], preferred_element_type=jnp.float32)
            result = result[0:COLS] + result[height : height + COLS]
            for y in range(cells_y):
                for c in range(0, COLS, 8):
                    where = (c * blocks + i) * cells_y + y
                    q_rows[pl.ds(where, 8, stride=blocks * cells_y), :] = result[
                        c : c + 8, y * 128 : (y + 1) * 128
                    ]
        save(n).start()
        return carry

    lax.fori_loop(0, blocks // group, some, 0)
    rows = jnp.dot(
        permutation(COLS, COLS), factor_ref[:, 0:COLS],
        precision=HIGHEST, preferred_element_type=jnp.float32,
    )
    factor = jnp.dot(rows, mixing(), precision=HIGHEST, preferred_element_type=jnp.float32)
    r_ref[...] = factor
    rms_ref[...] = jnp.sqrt(jnp.sum(factor * factor, axis=0, keepdims=True) / all_cells)
    for n in range(blocks // group):
        save(n).wait()


def orthonormal(all_cells, cells, parts, inverse, factor):
    cells_x, cells_y = cells
    blocks, depth, width = parts.shape
    group = 2
    height = 16 * PAIRS
    return pl.pallas_call(
        functools.partial(orthonormal_kernel, all_cells, cells_y, blocks, group),
        out_shape=(
            jax.ShapeDtypeStruct((COLS, blocks, cells_y, 128), jnp.float32),
            jax.ShapeDtypeStruct((COLS, COLS), jnp.float32),
            jax.ShapeDtypeStruct((1, COLS), jnp.float32),
        ),
        in_specs=[
            pl.BlockSpec(memory_space=pltpu.HBM),
            pl.BlockSpec(memory_space=VMEM),
            pl.BlockSpec(memory_space=VMEM),
        ],
        out_specs=(
            pl.BlockSpec(memory_space=pltpu.HBM),
            pl.BlockSpec(memory_space=VMEM),
            pl.BlockSpec(memory_space=VMEM),
        ),
        scratch_shapes=[
            VMEM((2 * height, depth), jnp.bfloat16),
            VMEM(parts.shape, jnp.bfloat16),
            VMEM((COLS, blocks, cells_y, 128), jnp.float32),
            pltpu.SemaphoreType.DMA((blocks // group,)),
            pltpu.SemaphoreType.DMA((blocks // group,)),
        ],
        compiler_params=pltpu.CompilerParams(vmem_limit_bytes=55 * 1024 * 1024),
        name="orthonormal",
    )(parts, inverse, factor)


def shards(actuator_mask, forcing, base_flow, base_shear):
    _, cells_x, cells_y, cells_z = base_flow.shape
    counts = (lax.axis_size("gx"), lax.axis_size("gy"))
    all_cells = 4.0 * cells_x * counts[0] * cells_y * counts[1] * cells_z
    rows, inverse, factor = basis(actuator_mask, forcing, base_flow, base_shear, counts)
    q_basis, r_factor, rms = orthonormal(all_cells, (cells_x, cells_y), rows, inverse, factor)
    return (q_basis.reshape(COLS, 4, cells_x, cells_y, cells_z), r_factor, rms[0])


def solution(mesh):
    return jax.shard_map(
        shards,
        mesh=mesh,
        in_specs=(
            P(None, "gx", "gy", None),
            P(None, None, "gx", "gy", None),
            P(None, "gx", "gy", None),
            P(None, None, "gx", "gy", None),
        ),
        out_specs=(P(None, None, "gx", "gy", None), P(), P()),
        check_vma=False,
    )
```
